256 devices in a mesh: row: 16 (over z_hi, x), col: 16 (over y, z_lo, core).
Axes of the slice: x: 4, y: 4, z: 8 (z_hi: 4, z_lo: 2; z = z_hi * 2 + z_lo), core: 2. Of those that a mesh axis runs over, the one named last changes fastest.
Arguments:
- right_side: float32 [64, 16, 4096], P(None, 'col', 'row'), may hold values from -24 to 24
- tile_values: bfloat16 [16, 16, 64, 256, 256], P('row', 'col'), may hold values from -0.5 to 0.5
- tile_rows: int32 [16, 16, 64], P('row', 'col'), may hold values from 0 to 15, as said below
- tile_cols: int32 [16, 16, 64], P('row', 'col'), may hold values from 0 to 7
- tile_count: int32 [16, 16], P('row', 'col'), may hold values from 32 to 64, as said below
Outputs:
- solution: float32 [64, 16, 2048], P(None, 'row', 'col')
- residual: float32 [64, 16, 4096], P(None, 'col', 'row')
The draws below stay inside these ranges and needn't reach their ends.
Inputs may be any that keep to these rules, and one draw needn't show every extreme that they name: `tile_rows`: within one device no two tiles share both tile row and tile column. The first tile_count tiles of a device's list belong to the matrix, the others are ignored.
All inputs are finite; a program needn't handle non-finite values.
Results may differ from the reference program's by a relative error of at most 0.013.
Values may be sent and summed in bfloat16 or wider, within the bound.
A program may use at most 64 MiB of HBM per device.

```python
import math
import jax
import jax.numpy as jnp
from jax import lax

RHS = 64
TILE = 256
RBG = 16
CBG = 8
TPD = 64
ITERS = 2
N_ROW = 16
N_COL = 16


def tile_slots(key):
    key_list = jax.random.split(key, N_ROW * N_COL)
    slot_ids = jax.vmap(lambda sub_key: jax.random.permutation(sub_key, RBG * CBG)[:TPD])(key_list)
    return slot_ids.reshape(N_ROW, N_COL, TPD).astype(jnp.int32)


def draw_tile_rows(key, part):
    slot_ids = tile_slots(key)
    return slot_ids // CBG


def draw_tile_cols(key, part):
    slot_ids = tile_slots(key)
    return slot_ids % CBG


def draw_tile_count(key, part):
    key = jax.random.fold_in(key, 7)
    count_key, pick_key = jax.random.split(key)
    device_total = N_ROW * N_COL
    counts = jax.random.randint(count_key, (device_total,), TPD // 2, TPD + 1)
    chosen = jax.random.randint(pick_key, (), 0, device_total)
    counts = counts.at[chosen].set(TPD)
    counts = counts.at[(chosen + 1) % device_total].set(TPD // 2)
    return counts.reshape(N_ROW, N_COL).astype(jnp.int32)


def draw_tile_values(key, part):
    key = jax.random.fold_in(key, 13)
    noise_key, offset_key = jax.random.split(key)
    shape_full = (N_ROW, N_COL, TPD, TILE, TILE)
    column_hits = TILE * N_COL * TPD * 3 // (4 * CBG)
    spread_scale = 1.0 / math.sqrt(column_hits)
    noise_values = jnp.clip(jax.random.normal(noise_key, shape_full, jnp.float32), -4.0, 4.0)
    tile_offset = jax.random.uniform(offset_key, (N_ROW, N_COL, TPD, 1, 1), jnp.float32, 0.0, 0.03)
    return ((noise_values + tile_offset) * spread_scale).astype(jnp.bfloat16)


def draw_right_side(key, part):
    key = jax.random.fold_in(key, 11)
    value_key = jax.random.fold_in(key, 0)
    row_key = jax.random.fold_in(key, 1)
    side_key = jax.random.fold_in(key, 2)
    offset_key = jax.random.fold_in(key, 4)
    sign_key = jax.random.fold_in(key, 5)
    shape_full = (RHS, N_COL, RBG * TILE)
    side_offset = jax.random.uniform(offset_key, (RHS, 1, 1), jnp.float32, 0.3, 0.6)
    offset_sign = jnp.where(jax.random.uniform(sign_key, (RHS, 1, 1), jnp.float32) < 0.5, -1.0, 1.0)
    side_offset = side_offset * offset_sign
    base_values = jax.random.normal(value_key, shape_full, jnp.float32)
    base_values = jnp.clip(base_values + side_offset, -4.0, 4.0)
    row_scale = jnp.exp(jax.random.uniform(row_key, (1, N_COL, RBG * TILE), jnp.float32, math.log(0.3), math.log(3.0)))
    side_scale = jnp.exp(jax.random.uniform(side_key, (RHS, 1, 1), jnp.float32, math.log(0.5), math.log(2.0)))
    return base_values * row_scale * side_scale


def setup_inputs(seed: int = 0) -> dict:
    seeds = jax.random.split(jax.random.key(seed), 6)
    right_side = draw_right_side(jax.random.fold_in(seeds[5], 71), 0)
    tile_values = draw_tile_values(jax.random.fold_in(seeds[5], 71), 0)
    tile_rows = draw_tile_rows(jax.random.fold_in(seeds[5], 71), 0)
    tile_cols = draw_tile_cols(jax.random.fold_in(seeds[5], 71), 0)
    tile_count = draw_tile_count(jax.random.fold_in(seeds[5], 71), 0)
    return {"right_side": right_side, "tile_values": tile_values, "tile_rows": tile_rows, "tile_cols": tile_cols, "tile_count": tile_count}


EPSILON = 1e-06
HIGHEST = lax.Precision.HIGHEST

def selectors(rows_list, cols_list, live_count):
    live_mask = (lax.iota(jnp.int32, rows_list.shape[0]) < live_count).astype(jnp.float32)
    row_hits = (rows_list[:, None] == lax.iota(jnp.int32, RBG)[None, :]).astype(jnp.float32)
    col_hits = (cols_list[:, None] == lax.iota(jnp.int32, CBG)[None, :]).astype(jnp.float32)
    return (row_hits, row_hits * live_mask[:, None], col_hits, col_hits * live_mask[:, None])

def forward_part(vector, tile_set, col_pick, row_add):
    sides = vector.shape[0]
    blocks = vector.reshape(sides, CBG, TILE).astype(jnp.float32)
    picked = jnp.einsum('tk,rkj->trj', col_pick, blocks, precision=HIGHEST)
    products = jnp.einsum('tij,trj->tri', tile_set.astype(jnp.float32), picked, precision=HIGHEST)
    summed = jnp.einsum('tb,tri->rbi', row_add, products, precision=HIGHEST)
    return summed.reshape(sides, RBG * TILE)

def backward_part(vector, tile_set, row_pick, col_add):
    sides = vector.shape[0]
    blocks = vector.reshape(sides, RBG, TILE).astype(jnp.float32)
    picked = jnp.einsum('tb,rbi->tri', row_pick, blocks, precision=HIGHEST)
    products = jnp.einsum('tij,tri->trj', tile_set.astype(jnp.float32), picked, precision=HIGHEST)
    summed = jnp.einsum('tk,trj->rkj', col_add, products, precision=HIGHEST)
    return summed.reshape(sides, CBG * TILE)

def apply_forward(vector, tile_values, tile_rows, tile_cols, tile_count):

    def add_device(total, position):
        row_group = position // N_COL
        col_group = position % N_COL
        row_pick, row_add, col_pick, col_add = selectors(tile_rows[row_group, col_group], tile_cols[row_group, col_group], tile_count[row_group, col_group])
        partial_sum = forward_part(vector[:, row_group], tile_values[row_group, col_group], col_pick, row_add)
        return (total.at[:, col_group].add(partial_sum), None)
    start_total = jnp.zeros((vector.shape[0], N_COL, RBG * TILE), jnp.float32)
    total, ignored = lax.scan(add_device, start_total, lax.iota(jnp.int32, N_ROW * N_COL))
    return total

def apply_backward(vector, tile_values, tile_rows, tile_cols, tile_count):

    def add_device(total, position):
        row_group = position // N_COL
        col_group = position % N_COL
        row_pick, row_add, col_pick, col_add = selectors(tile_rows[row_group, col_group], tile_cols[row_group, col_group], tile_count[row_group, col_group])
        partial_sum = backward_part(vector[:, col_group], tile_values[row_group, col_group], row_pick, col_add)
        return (total.at[:, row_group].add(partial_sum), None)
    start_total = jnp.zeros((vector.shape[0], N_ROW, CBG * TILE), jnp.float32)
    total, ignored = lax.scan(add_device, start_total, lax.iota(jnp.int32, N_ROW * N_COL))
    return total

def column_norm(vector):
    return jnp.sqrt(lax.optimization_barrier(jnp.sum(vector * vector, axis=(1, 2))) + EPSILON)

def spread(values):
    return values[:, None, None]

def reference(right_side, tile_values, tile_rows, tile_cols, tile_count):

    def forward(vector):
        return apply_forward(vector.astype(jnp.bfloat16), tile_values, tile_rows, tile_cols, tile_count)

    def backward(vector):
        return apply_backward(vector.astype(jnp.bfloat16), tile_values, tile_rows, tile_cols, tile_count)
    beta_norm = column_norm(right_side)
    left_vector = right_side / spread(beta_norm)
    backward_out = backward(right_side)
    right_raw = backward_out / spread(beta_norm)
    alpha_norm = column_norm(right_raw)
    right_vector = right_raw / spread(alpha_norm)
    search_dir = right_vector
    solution = jnp.zeros_like(right_vector)
    phi_bar = beta_norm
    rho_bar = alpha_norm
    for iteration in range(ITERS):
        forward_out = forward(right_raw)
        left_raw = forward_out / spread(alpha_norm) - spread(alpha_norm) * left_vector
        beta_norm = column_norm(left_raw)
        left_vector = left_raw / spread(beta_norm)
        backward_out = backward(left_raw)
        right_raw = backward_out / spread(beta_norm) - spread(beta_norm) * right_vector
        alpha_next = column_norm(right_raw)
        right_vector = right_raw / spread(alpha_next)
        rho_value = jnp.sqrt(rho_bar * rho_bar + beta_norm * beta_norm)
        cosine = rho_bar / rho_value
        sine_value = beta_norm / rho_value
        theta_value = sine_value * alpha_next
        rho_bar = -cosine * alpha_next
        phi_value = cosine * phi_bar
        phi_bar = sine_value * phi_bar
        solution = solution + spread(phi_value / rho_value) * search_dir
        search_dir = right_vector - spread(theta_value / rho_value) * search_dir
        alpha_norm = alpha_next
    residual = right_side - forward(solution)
    return (solution, residual)
```

```python
import functools

import jax
import jax.numpy as jnp
from jax import lax
from jax.experimental import pallas as pl
from jax.experimental.pallas import tpu as pltpu
from jax.sharding import PartitionSpec as P

MESH = pl.DeviceIdType.MESH
EPSILON = 1e-06
TILE = 256
PIECE = 128
NZ = 4


def order(i):
    return i + lax.div(i, 2) - 2 * lax.div(i, 3)


ORDER = {2: (0, 1), 4: (0, 1, 3, 2)}


def dot(a, b):
    return jnp.dot(a, b, preferred_element_type=jnp.float32)


def kernel(
    dims,
    rows_s,
    cols_s,
    count_s,
    rhs,
    tiles_hbm,
    sol_out,
    res_out,
    tiles,
    ttiles,
    idx_v,
    idx_s,
    zb,
    s1send,
    s1recv,
    s2send,
    s2recv,
    part,
    csend,
    crecv,
    wrecv,
    wfull,
    outp,
    first_f,
    nsend,
    nrecv,
    tile_sem,
    idx_sem,
    zb_send,
    zb_z,
    zb_x,
    s1_send,
    s1_sem,
    s2_send,
    s2_sem,
    c_send,
    c_sem,
    w_send,
    w_sem,
    n_send,
    n_sem,
):
    nz, nx, nc, cbg, tpd, sides = dims
    nr = nz * nx
    r = lax.axis_index("row")
    c = lax.axis_index("col")
    zh = lax.div(r, nx)
    x = lax.rem(r, nx)

    load = pltpu.make_async_copy(tiles_hbm.at[0, 0], tiles.at[pl.ds(0, tpd)], tile_sem)
    load.start()

    barrier = pltpu.get_barrier_semaphore()
    for d in range(1, nr):
        pl.semaphore_signal(barrier, inc=1, device_id=(lax.rem(r + d, nr), c), device_id_type=MESH)
    for d in range(1, nc):
        pl.semaphore_signal(barrier, inc=1, device_id=(r, lax.rem(c + d, nc)), device_id_type=MESH)

    def send(src, dst, send_sem, recv_sem, device):
        pltpu.make_async_remote_copy(
            src_ref=src,
            dst_ref=dst,
            send_sem=send_sem,
            recv_sem=recv_sem,
            device_id=device,
            device_id_type=MESH,
        ).start()

    def take(ref, sem):
        pltpu.make_async_copy(ref, ref, sem).wait()

    def x_peer(dx):
        return (zh * nx + lax.rem(x + dx, nx), c)

    def z_peer(dz):
        return (lax.rem(zh + dz, nz) * nx + x, c)

    eye = (
        lax.broadcasted_iota(jnp.int32, (sides, 128), 0)
        == lax.broadcasted_iota(jnp.int32, (sides, 128), 1)
    ).astype(jnp.float32)

    def to_row(column):
        return jnp.sum(column * eye, axis=0, keepdims=True)

    def to_column(row):
        return jnp.sum(row * eye, axis=1, keepdims=True)

    def square_sum(array):
        return to_row(jnp.sum(array * array, axis=1, keepdims=True))

    def norm_start(n, value, axis):
        nsend[n] = jnp.broadcast_to(value, (8, 128))
        for d in range(1, nr if axis == "row" else nc):
            device = (lax.rem(r + d, nr), c) if axis == "row" else (r, lax.rem(c + d, nc))
            send(nsend.at[n], nrecv.at[n, d], n_send.at[n], n_sem.at[n], device)

    def norm_finish(n, value, axis):
        size = nr if axis == "row" else nc
        take(nrecv.at[n, pl.ds(1, size - 1)], n_sem.at[n])
        for d in range(1, size):
            value = value + nrecv[n, d, 0:1, :]
        return value

    def make_index():
        lane = lax.broadcasted_iota(jnp.int32, (8, 128), 1)
        count = count_s[0, 0]

        def one(t, table):
            key = rows_s[0, 0, t] * cbg + cols_s[0, 0, t]
            key = jnp.where(t < count, key, -1)
            return jnp.where(lane == key, t, table)

        idx_v[...] = lax.fori_loop(0, tpd, one, jnp.full((8, 128), tpd, jnp.int32))
        copy = pltpu.make_async_copy(idx_v, idx_s, idx_sem)
        copy.start()
        copy.wait()

    def make_transposed():
        load.wait()
        tiles[tpd] = jnp.zeros((TILE, TILE), jnp.bfloat16)
        ttiles[tpd] = jnp.zeros((TILE, TILE), jnp.bfloat16)

        def some(step, carry):
            for u in range(4):
                ttiles[step * 4 + u] = tiles[step * 4 + u].T
            return carry

        lax.fori_loop(0, tpd // 4, some, 0)

    def backward(inst, vector, n, first):
        zb[inst, 0] = vector.astype(jnp.bfloat16)
        if first:
            pl.semaphore_wait(barrier, nr + nc - 2)
        for dz in reversed(ORDER[nz][1:]):
            send(zb.at[inst, 0], zb.at[inst, dz * nx], zb_send.at[inst], zb_z.at[inst, dz], z_peer(dz))
        for dx in reversed(ORDER[nx][1:]):
            send(zb.at[inst, 0], zb.at[inst, dx], zb_send.at[inst], zb_x.at[inst, 0], x_peer(dx))
        squares = square_sum(vector)
        norm_start(n, squares, "row")
        if first:
            make_index()
        for dz in ORDER[nz][1:]:
            take(zb.at[inst, dz * nx], zb_z.at[inst, dz])
            for dx in reversed(ORDER[nx][1:]):
                send(
                    zb.at[inst, dz * nx],
                    zb.at[inst, dz * nx + dx],
                    zb_send.at[inst],
                    zb_x.at[inst, dz],
                    x_peer(dx),
                )
        if first:
            make_transposed()
        for piece in range(nc):
            outp[piece] = jnp.zeros((sides, PIECE), jnp.float32)

        def group(i, carry):
            dz = order(i)
            take(zb.at[inst, pl.ds(dz * nx + 1, nx - 1)], zb_x.at[inst, dz])
            origin = lax.rem(zh - dz + nz, nz) * nx
            for k in range(cbg):
                total = None
                for dx in range(nx):
                    block = origin + lax.rem(x - dx + nx, nx)
                    product = dot(zb[inst, dz * nx + dx], tiles[idx_s[0, block * cbg + k]])
                    total = product if total is None else total + product
                outp[2 * k] += total[:, :PIECE]
                outp[2 * k + 1] += total[:, PIECE:]
            return carry

        lax.fori_loop(0, nz, group, 0)
        squares = norm_finish(n, squares, "row")
        norm_start(n + 1, squares, "col")
        for d in range(1, nc):
            peer = lax.rem(c + d, nc)
            csend[inst, d] = outp[peer].astype(jnp.bfloat16)
            send(csend.at[inst, d], crecv.at[inst, d], c_send.at[inst], c_sem.at[inst], (r, peer))
        total = outp[c]
        take(crecv.at[inst, pl.ds(1, nc - 1)], c_sem.at[inst])
        for d in range(1, nc):
            total = total + crecv[inst, d].astype(jnp.float32)
        squares = norm_finish(n + 1, squares, "col")
        return total, jnp.sqrt(to_column(squares) + EPSILON)

    def forward(inst, vector, n):
        wrecv[inst, 0] = vector.astype(jnp.bfloat16)
        for d in range(1, nc):
            send(
                wrecv.at[inst, 0],
                wrecv.at[inst, d],
                w_send.at[inst],
                w_sem.at[inst],
                (r, lax.rem(c + d, nc)),
            )
        squares = square_sum(vector)
        norm_start(n, squares, "col")
        take(wrecv.at[inst, pl.ds(1, nc - 1)], w_sem.at[inst])
        for k in range(cbg):
            wfull[k, :, :PIECE] = wrecv[inst, lax.rem(c - 2 * k + nc, nc)]
            wfull[k, :, PIECE:] = wrecv[inst, lax.rem(c - 2 * k - 1 + nc, nc)]

        def group(i, carry):
            dz = order(nz - 1 - i)
            for dx in reversed(ORDER[nx]):
                block = lax.rem(zh + dz, nz) * nx + lax.rem(x + dx, nx)
                total = None
                for k in range(cbg):
                    product = dot(wfull[k], ttiles[idx_s[0, block * cbg + k]])
                    total = product if total is None else total + product
                if dx == 0:
                    part[dz] = total
                else:
                    slot = dz * nx + dx
                    s1send[inst, slot] = total.astype(jnp.bfloat16)
                    send(
                        s1send.at[inst, slot],
                        s1recv.at[inst, slot],
                        s1_send.at[inst],
                        s1_sem.at[inst, dz],
                        x_peer(dx),
                    )
            return carry

        lax.fori_loop(0, nz, group, 0)
        squares = norm_finish(n, squares, "col")
        norm_start(n + 1, squares, "row")
        total = None
        for dz in reversed(ORDER[nz]):
            take(s1recv.at[inst, pl.ds(dz * nx + 1, nx - 1)], s1_sem.at[inst, dz])
            total = part[dz]
            for dx in range(1, nx):
                total = total + s1recv[inst, dz * nx + dx].astype(jnp.float32)
            if dz:
                s2send[inst, dz] = total.astype(jnp.bfloat16)
                send(
                    s2send.at[inst, dz],
                    s2recv.at[inst, dz],
                    s2_send.at[inst],
                    s2_sem.at[inst],
                    z_peer(dz),
                )
        take(s2recv.at[inst, pl.ds(1, nz - 1)], s2_sem.at[inst])
        for dz in range(1, nz):
            total = total + s2recv[inst, dz].astype(jnp.float32)
        squares = norm_finish(n + 1, squares, "row")
        return total, jnp.sqrt(to_column(squares) + EPSILON)

    begin = rhs[...]
    back, beta0 = backward(0, begin, 0, True)
    right_raw = back / beta0
    forward1, alpha0 = forward(0, right_raw, 2)
    first_f[...] = forward1
    right0 = right_raw / alpha0
    left_raw = forward1 / alpha0 - alpha0 * (begin / beta0)
    back, beta1 = backward(1, left_raw, 4, False)
    right_raw = back / beta1 - beta1 * right0
    forward2, alpha1 = forward(1, right_raw, 6)
    right1 = right_raw / alpha1
    left_raw = forward2 / alpha1 - alpha1 * (left_raw / beta1)

    squares = square_sum(left_raw)
    norm_start(8, squares, "row")
    rho_bar = alpha0
    phi_bar = beta0
    rho_value = jnp.sqrt(rho_bar * rho_bar + beta1 * beta1)
    cosine = rho_bar / rho_value
    sine_value = beta1 / rho_value
    theta_value = sine_value * alpha1
    step0 = cosine * phi_bar / rho_value
    turn0 = theta_value / rho_value
    rho_bar = -cosine * alpha1
    phi_bar = sine_value * phi_bar
    squares = norm_finish(8, squares, "row")
    norm_start(9, squares, "col")
    squares = norm_finish(9, squares, "col")
    beta2 = jnp.sqrt(to_column(squares) + EPSILON)
    rho_value = jnp.sqrt(rho_bar * rho_bar + beta2 * beta2)
    step1 = rho_bar / rho_value * phi_bar / rho_value
    weight0 = step0 - step1 * turn0
    sol_out[...] = weight0 * right0 + step1 * right1
    res_out[...] = begin - (weight0 / alpha0) * first_f[...] - (step1 / alpha1) * forward2

    for inst in range(2):
        take(zb.at[inst, pl.ds(1, nr - 1)], zb_send.at[inst])
        take(s1recv.at[inst, pl.ds(0, nz * (nx - 1))], s1_send.at[inst])
        take(s2recv.at[inst, pl.ds(1, nz - 1)], s2_send.at[inst])
        take(crecv.at[inst, pl.ds(1, nc - 1)], c_send.at[inst])
        take(wrecv.at[inst, pl.ds(1, nc - 1)], w_send.at[inst])
    for n in range(10):
        size = nr if n in (0, 3, 4, 7, 8) else nc
        take(nrecv.at[n, pl.ds(1, size - 1)], n_send.at[n])


def local(dims, right_side, tile_values, tile_rows, tile_cols, tile_count):
    nz, nx, nc, cbg, tpd, sides = dims
    nr = nz * nx
    bf16, f32, i32 = jnp.bfloat16, jnp.float32, jnp.int32
    smem = pl.BlockSpec(memory_space=pltpu.SMEM)
    vmem = pl.BlockSpec(memory_space=pltpu.VMEM)
    dma = pltpu.SemaphoreType.DMA
    solution, residual = pl.pallas_call(
        functools.partial(kernel, dims),
        out_shape=(
            jax.ShapeDtypeStruct((sides, PIECE), f32),
            jax.ShapeDtypeStruct((sides, TILE), f32),
        ),
        in_specs=[smem, smem, smem, vmem, pl.BlockSpec(memory_space=pl.ANY)],
        out_specs=(vmem, vmem),
        scratch_shapes=[
            pltpu.VMEM((tpd + 1, TILE, TILE), bf16),
            pltpu.VMEM((tpd + 1, TILE, TILE), bf16),
            pltpu.VMEM((8, 128), i32),
            pltpu.SMEM((8, 128), i32),
            pltpu.VMEM((2, nr, sides, TILE), bf16),
            pltpu.VMEM((2, nr, sides, TILE), bf16),
            pltpu.VMEM((2, nr, sides, TILE), bf16),
            pltpu.VMEM((2, nz, sides, TILE), bf16),
            pltpu.VMEM((2, nz, sides, TILE), bf16),
            pltpu.VMEM((nz, sides, TILE), f32),
            pltpu.VMEM((2, nc, sides, PIECE), bf16),
            pltpu.VMEM((2, nc, sides, PIECE), bf16),
            pltpu.VMEM((2, nc, sides, PIECE), bf16),
            pltpu.VMEM((cbg, sides, TILE), bf16),
            pltpu.VMEM((nc, sides, PIECE), f32),
            pltpu.VMEM((sides, TILE), f32),
            pltpu.VMEM((10, 8, 128), f32),
            pltpu.VMEM((10, max(nr, nc), 8, 128), f32),
            dma,
            dma,
            dma((2,)),
            dma((2, nz)),
            dma((2, nz)),
            dma((2,)),
            dma((2, nz)),
            dma((2,)),
            dma((2,)),
            dma((2,)),
            dma((2,)),
            dma((2,)),
            dma((2,)),
            dma((10,)),
            dma((10,)),
        ],
        compiler_params=pltpu.CompilerParams(
            collective_id=0, has_side_effects=True, vmem_limit_bytes=48 * 2**20
        ),
        name="lsqr",
    )(tile_rows, tile_cols, tile_count, right_side[:, 0, :], tile_values)
    return solution.reshape(sides, 1, PIECE), residual.reshape(sides, 1, TILE)


def solution(mesh):
    in_specs = (
        P(None, "col", "row"),
        P("row", "col", None, None, None),
        P("row", "col", None),
        P("row", "col", None),
        P("row", "col"),
    )
    out_specs = (P(None, "row", "col"), P(None, "col", "row"))
    nr, nc = mesh.shape["row"], mesh.shape["col"]
    nz = 4 if nr == 16 else 2

    def program(right_side, tile_values, tile_rows, tile_cols, tile_count):
        dims = (nz, nr // nz, nc, nc * PIECE // TILE, tile_values.shape[2], right_side.shape[0])
        return jax.shard_map(
            functools.partial(local, dims),
            mesh=mesh,
            in_specs=in_specs,
            out_specs=out_specs,
            check_vma=False,
        )(right_side, tile_values, tile_rows, tile_cols, tile_count)

    return program
```

```python
import functools
import itertools

import jax
import jax.numpy as jnp
from jax import lax
from jax.experimental import pallas as pl
from jax.experimental.pallas import tpu as pltpu
from jax.sharding import PartitionSpec as P

MESH = pl.DeviceIdType.MESH
EPSILON = 1e-06
TILE = 256
PIECE = 128
NZ = 4


def order(i):
    return i + lax.div(i, 2) - 2 * lax.div(i, 3)


ORDER = {2: (0, 1), 4: (0, 1, 3, 2)}


def dot(a, b):
    return jnp.dot(a, b, preferred_element_type=jnp.float32)


def kernel(
    dims,
    rows_hbm,
    cols_hbm,
    count_hbm,
    rhs_hbm,
    tiles_hbm,
    sol_out,
    res_out,
    rows_s,
    cols_s,
    count_s,
    rhs,
    tiles,
    ttiles,
    idx_v,
    idx_s,
    zb,
    s1send,
    s1recv,
    s2send,
    s2recv,
    part,
    csend,
    crecv,
    wrecv,
    wfull,
    outp,
    first_f,
    nsend,
    nrecv,
    frecv,
    tile_sem,
    small_sem,
    rhs_sem,
    idx_sem,
    zb_send,
    zb_z,
    zb_x,
    s1_send,
    s1_sem,
    s2_send,
    s2_sem,
    c_send,
    c_sem,
    w_send,
    w_sem,
    n_send,
    n_sem,
):
    nz, nx, nc, cbg, tpd, sides = dims
    nr = nz * nx
    ny = nc // 4
    r = lax.axis_index("row")
    c = lax.axis_index("col")
    zh = lax.div(r, nx)
    x = lax.rem(r, nx)

    load = pltpu.make_async_copy(tiles_hbm.at[0, 0], tiles.at[pl.ds(0, tpd)], tile_sem)
    load.start()
    small = [
        pltpu.make_async_copy(rows_hbm, rows_s, small_sem.at[0]),
        pltpu.make_async_copy(cols_hbm, cols_s, small_sem.at[1]),
        pltpu.make_async_copy(count_hbm, count_s, small_sem.at[2]),
        pltpu.make_async_copy(rhs_hbm.at[:, 0, :], rhs, rhs_sem),
    ]
    for copy in small:
        copy.start()

    barrier = pltpu.get_barrier_semaphore()

    def x_peer(dx):
        return (zh * nx + lax.rem(x + dx, nx), c)

    def z_peer(dz):
        return (lax.rem(zh + dz, nz) * nx + x, c)

    def at_offset(offset, dc):
        z = lax.rem(2 * zh + lax.rem(lax.div(c, 2), 2) + offset[0], 2 * nz)
        y = lax.rem(lax.div(c, 4) + offset[2], ny)
        core = lax.rem(lax.rem(c, 2) + dc, 2)
        return (
            lax.div(z, 2) * nx + lax.rem(x + offset[1], nx),
            y * 4 + lax.rem(z, 2) * 2 + core,
        )

    sizes = (2 * nz, nx, ny)
    offsets = sorted(
        itertools.product(*map(range, sizes)),
        key=lambda o: -sum(min(d, s - d) for d, s in zip(o, sizes)),
    )
    peers = {
        "x": [x_peer(dx) for dx in range(1, nx)],
        "z": [z_peer(dz) for dz in range(1, nz)],
        "row": [(lax.rem(r + d, nr), c) for d in range(1, nr)],
        "col": [(r, lax.rem(c + d, nc)) for d in range(1, nc)],
        "core": [at_offset((0, 0, 0), 1)],
        "chips": [at_offset(o, 0) for o in offsets if any(o)],
    }
    greeted = peers["z"] + peers["x"] + peers["col"]
    for device in greeted:
        pl.semaphore_signal(barrier, inc=1, device_id=device, device_id_type=MESH)

    def send(src, dst, send_sem, recv_sem, device):
        pltpu.make_async_remote_copy(
            src_ref=src,
            dst_ref=dst,
            send_sem=send_sem,
            recv_sem=recv_sem,
            device_id=device,
            device_id_type=MESH,
        ).start()

    def take(ref, sem):
        pltpu.make_async_copy(ref, ref, sem).wait()

    eye = (
        lax.broadcasted_iota(jnp.int32, (sides, 128), 0)
        == lax.broadcasted_iota(jnp.int32, (sides, 128), 1)
    ).astype(jnp.float32)

    def to_row(column):
        return jnp.sum(column * eye, axis=0, keepdims=True)

    def to_column(row):
        return jnp.sum(row * eye, axis=1, keepdims=True)

    def square_sum(array):
        return to_row(jnp.sum(array * array, axis=1, keepdims=True))

    def norm_start(n, value, kind):
        nsend[pl.ds(n, 1), :] = value
        slots = frecv if kind == "chips" else nrecv.at[n]
        for d, device in enumerate(peers[kind]):
            send(nsend.at[pl.ds(n, 1)], slots.at[pl.ds(d, 1)], n_send.at[n], n_sem.at[n], device)

    def norm_finish(n, value, kind):
        slots = frecv if kind == "chips" else nrecv.at[n]
        size = len(peers[kind])
        take(slots.at[pl.ds(0, size)], n_sem.at[n])
        return value + jnp.sum(slots[0:size, :], axis=0, keepdims=True)

    def make_index():
        lane = lax.broadcasted_iota(jnp.int32, (8, 128), 1)
        count = count_s[0, 0]

        def one(t, table):
            key = rows_s[0, 0, t] * cbg + cols_s[0, 0, t]
            key = jnp.where(t < count, key, -1)
            return jnp.where(lane == key, t, table)

        idx_v[...] = lax.fori_loop(0, tpd, one, jnp.full((8, 128), tpd, jnp.int32))
        copy = pltpu.make_async_copy(idx_v, idx_s, idx_sem)
        copy.start()
        copy.wait()

    def make_transposed(begin, end):
        def some(step, carry):
            for u in range(4):
                ttiles[step * 4 + u] = tiles[step * 4 + u].T
            return carry

        lax.fori_loop(begin // 4, end // 4, some, 0)

    def backward(inst, vector, prepare, first):
        zb[inst, 0] = vector.astype(jnp.bfloat16)
        squares = square_sum(vector) if first else None
        if first:
            tiles[tpd] = jnp.zeros((TILE, TILE), jnp.bfloat16)
            ttiles[tpd] = jnp.zeros((TILE, TILE), jnp.bfloat16)
            load.wait()
            make_transposed(0, tpd // 2)
            pl.semaphore_wait(barrier, len(greeted))
        for dz in reversed(ORDER[nz][1:]):
            send(zb.at[inst, 0], zb.at[inst, dz * nx], zb_send.at[inst], zb_z.at[inst, dz], z_peer(dz))
        for dx in reversed(ORDER[nx][1:]):
            send(zb.at[inst, 0], zb.at[inst, dx], zb_send.at[inst], zb_x.at[inst, 0], x_peer(dx))
        if first:
            norm_start(0, squares, "z")
        else:
            squares = square_sum(vector)
            norm_start(3, squares, "row")
        for piece in range(nc):
            outp[piece] = jnp.zeros((sides, PIECE), jnp.float32)
        if first:
            make_index()
        for dz in ORDER[nz][1:]:
            take(zb.at[inst, dz * nx], zb_z.at[inst, dz])
            for dx in reversed(ORDER[nx][1:]):
                send(
                    zb.at[inst, dz * nx],
                    zb.at[inst, dz * nx + dx],
                    zb_send.at[inst],
                    zb_x.at[inst, dz],
                    x_peer(dx),
                )
        if first:
            squares = norm_finish(0, squares, "z")
            norm_start(1, squares, "x")
            make_transposed(tpd // 2, tpd)

        def group(i, carry):
            dz = order(i)
            take(zb.at[inst, pl.ds(dz * nx + 1, nx - 1)], zb_x.at[inst, dz])
            origin = lax.rem(zh - dz + nz, nz) * nx
            for k in range(cbg):
                total = None
                for dx in range(nx):
                    block = origin + lax.rem(x - dx + nx, nx)
                    product = dot(zb[inst, dz * nx + dx], tiles[idx_s[0, block * cbg + k]])
                    total = product if total is None else total + product
                outp[2 * k] += total[:, :PIECE]
                outp[2 * k + 1] += total[:, PIECE:]
            return carry

        lax.fori_loop(0, nz - 1, group, 0)
        squares = norm_finish(1, squares, "x") if first else norm_finish(3, squares, "row")
        n = 2 if first else 4
        norm_start(n, squares, "col")
        group(nz - 1, 0)
        for d in sorted(range(1, nc), key=lambda d: -min(d, nc - d)):
            peer = lax.rem(c + d, nc)
            csend[inst, d] = outp[peer].astype(jnp.bfloat16)
            send(csend.at[inst, d], crecv.at[inst, d], c_send.at[inst], c_sem.at[inst], (r, peer))
        squares = norm_finish(n, squares, "col")
        norm = jnp.sqrt(to_column(squares) + EPSILON)
        prepared = prepare(norm)
        take(crecv.at[inst, pl.ds(1, nc - 1)], c_sem.at[inst])
        total = outp[c]
        for d in range(1, nc):
            total = total + crecv[inst, d].astype(jnp.float32)
        return total, norm, prepared

    def forward(inst, vector, n, prepare):
        wrecv[inst, 0] = vector.astype(jnp.bfloat16)
        for d in sorted(range(1, nc), key=lambda d: -min(d, nc - d)):
            send(
                wrecv.at[inst, 0],
                wrecv.at[inst, d],
                w_send.at[inst],
                w_sem.at[inst],
                (r, lax.rem(c + d, nc)),
            )
        squares = square_sum(vector)
        norm_start(n, squares, "col")
        take(wrecv.at[inst, pl.ds(1, nc - 1)], w_sem.at[inst])
        for k in range(cbg):
            wfull[k, :, :PIECE] = wrecv[inst, lax.rem(c - 2 * k + nc, nc)]
            wfull[k, :, PIECE:] = wrecv[inst, lax.rem(c - 2 * k - 1 + nc, nc)]

        def group(i, carry):
            dz = order(nz - 1 - i)
            for dx in reversed(ORDER[nx]):
                block = lax.rem(zh + dz, nz) * nx + lax.rem(x + dx, nx)
                total = None
                for k in range(cbg):
                    product = dot(wfull[k], ttiles[idx_s[0, block * cbg + k]])
                    total = product if total is None else total + product
                if dx == 0:
                    part[dz] = total
                else:
                    slot = dz * nx + dx
                    s1send[inst, slot] = total.astype(jnp.bfloat16)
                    send(
                        s1send.at[inst, slot],
                        s1recv.at[inst, slot],
                        s1_send.at[inst],
                        s1_sem.at[inst, dz],
                        x_peer(dx),
                    )
            return carry

        group(0, 0)
        squares = norm_finish(n, squares, "col")
        norm_start(n + 1, squares, "row")
        lax.fori_loop(1, nz, group, 0)
        total = None
        for dz in reversed(ORDER[nz]):
            take(s1recv.at[inst, pl.ds(dz * nx + 1, nx - 1)], s1_sem.at[inst, dz])
            total = part[dz]
            for dx in range(1, nx):
                total = total + s1recv[inst, dz * nx + dx].astype(jnp.float32)
            if dz:
                s2send[inst, dz] = total.astype(jnp.bfloat16)
                send(
                    s2send.at[inst, dz],
                    s2recv.at[inst, dz],
                    s2_send.at[inst],
                    s2_sem.at[inst],
                    z_peer(dz),
                )
        squares = norm_finish(n + 1, squares, "row")
        norm = jnp.sqrt(to_column(squares) + EPSILON)
        prepared = prepare(norm)
        take(s2recv.at[inst, pl.ds(1, nz - 1)], s2_sem.at[inst])
        for dz in range(1, nz):
            total = total + s2recv[inst, dz].astype(jnp.float32)
        return total, norm, prepared

    for copy in small:
        copy.wait()
    back, beta0, scale = backward(0, rhs[...], lambda norm: 1.0 / norm, True)
    right_raw0 = back * scale
    forward1, alpha0, (scale, shift) = forward(
        0, right_raw0, 5, lambda norm: (1.0 / norm, (norm / beta0) * rhs[...])
    )
    left_raw1 = forward1 * scale - shift
    first_f[...] = forward1
    back, beta1, (scale, shift) = backward(
        1, left_raw1, lambda norm: (1.0 / norm, (norm / alpha0) * right_raw0), False
    )
    right_raw1 = back * scale - shift
    forward2, alpha1, (scale, shift) = forward(
        1, right_raw1, 7, lambda norm: (1.0 / norm, (norm / beta1) * left_raw1)
    )
    left_raw2 = forward2 * scale - shift

    squares = square_sum(left_raw2)
    norm_start(9, squares, "core")
    squares = norm_finish(9, squares, "core")
    norm_start(10, squares, "chips")
    rho_bar = alpha0
    phi_bar = beta0
    rho_value = jnp.sqrt(rho_bar * rho_bar + beta1 * beta1)
    cosine = rho_bar / rho_value
    sine_value = beta1 / rho_value
    theta_value = sine_value * alpha1
    step0 = cosine * phi_bar / rho_value
    turn0 = theta_value / rho_value
    rho_bar = -cosine * alpha1
    phi_bar = sine_value * phi_bar
    squares = norm_finish(10, squares, "chips")
    beta2 = jnp.sqrt(to_column(squares) + EPSILON)
    rho_value = jnp.sqrt(rho_bar * rho_bar + beta2 * beta2)
    step1 = rho_bar / rho_value * phi_bar / rho_value
    weight0 = step0 - step1 * turn0
    weight0 = weight0 / alpha0
    weight1 = step1 / alpha1
    sol_out[...] = weight0 * right_raw0 + weight1 * right_raw1
    res_out[...] = rhs[...] - weight0 * first_f[...] - weight1 * forward2

    for inst in range(2):
        take(zb.at[inst, pl.ds(1, nr - 1)], zb_send.at[inst])
        take(s1recv.at[inst, pl.ds(0, nz * (nx - 1))], s1_send.at[inst])
        take(s2recv.at[inst, pl.ds(1, nz - 1)], s2_send.at[inst])
        take(crecv.at[inst, pl.ds(1, nc - 1)], c_send.at[inst])
        take(wrecv.at[inst, pl.ds(1, nc - 1)], w_send.at[inst])
    kinds = ("z", "x", "col", "row", "col", "col", "row", "col", "row", "core")
    for n, kind in enumerate(kinds):
        take(nrecv.at[n, pl.ds(0, len(peers[kind]))], n_send.at[n])
    take(frecv.at[pl.ds(0, len(peers["chips"]))], n_send.at[10])


def place(solution, residual, sol_out, res_out):
    sol_out[:, 0, :] = solution[...]
    res_out[:, 0, :] = residual[...]


def local(dims, right_side, tile_values, tile_rows, tile_cols, tile_count):
    nz, nx, nc, cbg, tpd, sides = dims
    nr = nz * nx
    bf16, f32, i32 = jnp.bfloat16, jnp.float32, jnp.int32
    vmem = pl.BlockSpec(memory_space=pltpu.VMEM)
    dma = pltpu.SemaphoreType.DMA
    solution, residual = pl.pallas_call(
        functools.partial(kernel, dims),
        out_shape=(
            jax.ShapeDtypeStruct((sides, PIECE), f32),
            jax.ShapeDtypeStruct((sides, TILE), f32),
        ),
        in_specs=[pl.BlockSpec(memory_space=pltpu.HBM)] * 5,
        out_specs=(vmem, vmem),
        scratch_shapes=[
            pltpu.SMEM((1, 1, tpd), i32),
            pltpu.SMEM((1, 1, tpd), i32),
            pltpu.SMEM((1, 1), i32),
            pltpu.VMEM((sides, TILE), f32),
            pltpu.VMEM((tpd + 1, TILE, TILE), bf16),
            pltpu.VMEM((tpd + 1, TILE, TILE), bf16),
            pltpu.VMEM((8, 128), i32),
            pltpu.SMEM((8, 128), i32),
            pltpu.VMEM((2, nr, sides, TILE), bf16),
            pltpu.VMEM((2, nr, sides, TILE), bf16),
            pltpu.VMEM((2, nr, sides, TILE), bf16),
            pltpu.VMEM((2, nz, sides, TILE), bf16),
            pltpu.VMEM((2, nz, sides, TILE), bf16),
            pltpu.VMEM((nz, sides, TILE), f32),
            pltpu.VMEM((2, nc, sides, PIECE), bf16),
            pltpu.VMEM((2, nc, sides, PIECE), bf16),
            pltpu.VMEM((2, nc, sides, PIECE), bf16),
            pltpu.VMEM((cbg, sides, TILE), bf16),
            pltpu.VMEM((nc, sides, PIECE), f32),
            pltpu.VMEM((sides, TILE), f32),
            pltpu.VMEM((16, 128), f32),
            pltpu.VMEM((10, max(nr, nc), 128), f32),
            pltpu.VMEM((nr * nc // 2, 128), f32),
            dma,
            dma((3,)),
            dma,
            dma,
            dma((2,)),
            dma((2, nz)),
            dma((2, nz)),
            dma((2,)),
            dma((2, nz)),
            dma((2,)),
            dma((2,)),
            dma((2,)),
            dma((2,)),
            dma((2,)),
            dma((2,)),
            dma((11,)),
            dma((11,)),
        ],
        compiler_params=pltpu.CompilerParams(
            collective_id=0, has_side_effects=True, vmem_limit_bytes=62 * 2**20
        ),
        name="lsqr",
    )(tile_rows, tile_cols, tile_count, right_side, tile_values)
    return pl.pallas_call(
        place,
        out_shape=(
            jax.ShapeDtypeStruct((sides, 1, PIECE), f32),
            jax.ShapeDtypeStruct((sides, 1, TILE), f32),
        ),
        in_specs=[vmem, vmem],
        out_specs=(vmem, vmem),
        name="place",
    )(solution, residual)


def solution(mesh):
    in_specs = (
        P(None, "col", "row"),
        P("row", "col", None, None, None),
        P("row", "col", None),
        P("row", "col", None),
        P("row", "col"),
    )
    out_specs = (P(None, "row", "col"), P(None, "col", "row"))
    nr, nc = mesh.shape["row"], mesh.shape["col"]
    nz = 4 if nr == 16 else 2

    def program(right_side, tile_values, tile_rows, tile_cols, tile_count):
        dims = (nz, nr // nz, nc, nc * PIECE // TILE, tile_values.shape[2], right_side.shape[0])
        return jax.shard_map(
            functools.partial(local, dims),
            mesh=mesh,
            in_specs=in_specs,
            out_specs=out_specs,
            check_vma=False,
        )(right_side, tile_values, tile_rows, tile_cols, tile_count)

    return program
```

```python
import functools
import itertools

import jax
import jax.numpy as jnp
from jax import lax
from jax.experimental import pallas as pl
from jax.experimental.pallas import tpu as pltpu
from jax.sharding import PartitionSpec as P

MESH = pl.DeviceIdType.MESH
EPSILON = 1e-06
TILE = 256
PIECE = 128
BACK_BATCH = 2
FORWARD_BATCH = 2


def order(i):
    return i + lax.div(i, 2) - 2 * lax.div(i, 3)


ORDER = {2: (0, 1), 4: (0, 1, 3, 2)}


def batches(items, size):
    return [items[i : i + size] for i in range(0, len(items), size)]


def dot(a, b):
    return jnp.dot(a, b, preferred_element_type=jnp.float32)


def kernel(
    dims,
    rows_hbm,
    cols_hbm,
    count_hbm,
    rhs_hbm,
    tiles_hbm,
    sol_out,
    res_out,
    rows_s,
    cols_s,
    count_s,
    rhs,
    tiles,
    ttiles,
    idx_v,
    idx_s,
    zb,
    s1send,
    s1recv,
    s2send,
    s2recv,
    part,
    csend,
    crecv,
    wrecv,
    wfull,
    outp,
    first_f,
    nsend,
    nrecv,
    frecv,
    tile_sem,
    small_sem,
    rhs_sem,
    idx_sem,
    zb_send,
    zb_z,
    zb_x,
    s1_send,
    s1_sem,
    s2_send,
    s2_sem,
    c_send,
    c_sem,
    w_send,
    w_sem,
    n_send,
    n_sem,
):
    nz, nx, nc, cbg, tpd, sides = dims
    nr = nz * nx
    ny = nc // 4
    r = lax.axis_index("row")
    c = lax.axis_index("col")
    zh = lax.div(r, nx)
    x = lax.rem(r, nx)

    load = pltpu.make_async_copy(tiles_hbm.at[0, 0], tiles.at[pl.ds(0, tpd)], tile_sem)
    load.start()
    small = [
        pltpu.make_async_copy(rows_hbm, rows_s, small_sem.at[0]),
        pltpu.make_async_copy(cols_hbm, cols_s, small_sem.at[1]),
        pltpu.make_async_copy(count_hbm, count_s, small_sem.at[2]),
        pltpu.make_async_copy(rhs_hbm.at[:, 0, :], rhs, rhs_sem),
    ]
    for copy in small:
        copy.start()

    barrier = pltpu.get_barrier_semaphore()

    def x_peer(dx):
        return (zh * nx + lax.rem(x + dx, nx), c)

    def z_peer(dz):
        return (lax.rem(zh + dz, nz) * nx + x, c)

    def at_offset(offset, dc):
        z = lax.rem(2 * zh + lax.rem(lax.div(c, 2), 2) + offset[0], 2 * nz)
        y = lax.rem(lax.div(c, 4) + offset[2], ny)
        core = lax.rem(lax.rem(c, 2) + dc, 2)
        return (
            lax.div(z, 2) * nx + lax.rem(x + offset[1], nx),
            y * 4 + lax.rem(z, 2) * 2 + core,
        )

    sizes = (2 * nz, nx, ny)
    offsets = sorted(
        itertools.product(*map(range, sizes)),
        key=lambda o: -sum(min(d, s - d) for d, s in zip(o, sizes)),
    )
    peers = {
        "x": [x_peer(dx) for dx in range(1, nx)],
        "z": [z_peer(dz) for dz in range(1, nz)],
        "row": [(lax.rem(r + d, nr), c) for d in range(1, nr)],
        "col": [(r, lax.rem(c + d, nc)) for d in range(1, nc)],
        "core": [at_offset((0, 0, 0), 1)],
        "chips": [at_offset(o, 0) for o in offsets if any(o)],
    }
    greeted = peers["z"] + peers["x"] + peers["col"]
    for device in greeted:
        pl.semaphore_signal(barrier, inc=1, device_id=device, device_id_type=MESH)

    def send(src, dst, send_sem, recv_sem, device):
        pltpu.make_async_remote_copy(
            src_ref=src,
            dst_ref=dst,
            send_sem=send_sem,
            recv_sem=recv_sem,
            device_id=device,
            device_id_type=MESH,
        ).start()

    def take(ref, sem):
        pltpu.make_async_copy(ref, ref, sem).wait()

    eye = (
        lax.broadcasted_iota(jnp.int32, (sides, 128), 0)
        == lax.broadcasted_iota(jnp.int32, (sides, 128), 1)
    ).astype(jnp.float32)

    def to_row(column):
        return jnp.sum(column * eye, axis=0, keepdims=True)

    def to_column(row):
        return jnp.sum(row * eye, axis=1, keepdims=True)

    def square_sum(array):
        return to_row(jnp.sum(array * array, axis=1, keepdims=True))

    def norm_start(n, value, kind):
        nsend[pl.ds(n, 1), :] = value
        slots = frecv if kind == "chips" else nrecv.at[n]
        for d, device in enumerate(peers[kind]):
            send(nsend.at[pl.ds(n, 1)], slots.at[pl.ds(d, 1)], n_send.at[n], n_sem.at[n], device)

    def norm_finish(n, value, kind):
        slots = frecv if kind == "chips" else nrecv.at[n]
        size = len(peers[kind])
        take(slots.at[pl.ds(0, size)], n_sem.at[n])
        return value + jnp.sum(slots[0:size, :], axis=0, keepdims=True)

    def make_index():
        lane = lax.broadcasted_iota(jnp.int32, (8, 128), 1)
        count = count_s[0, 0]

        def one(t, table):
            key = rows_s[0, 0, t] * cbg + cols_s[0, 0, t]
            key = jnp.where(t < count, key, -1)
            return jnp.where(lane == key, t, table)

        idx_v[...] = lax.fori_loop(0, tpd, one, jnp.full((8, 128), tpd, jnp.int32))
        copy = pltpu.make_async_copy(idx_v, idx_s, idx_sem)
        copy.start()
        copy.wait()

    def make_transposed(begin, end):
        def some(step, carry):
            for u in range(4):
                ttiles[step * 4 + u] = tiles[step * 4 + u].T
            return carry

        lax.fori_loop(begin // 4, end // 4, some, 0)

    chips = sorted(
        itertools.product(range(ny), range(2)), key=lambda o: (min(o[0], ny - o[0]), o[1])
    )
    core = lax.rem(c, 2)

    def chip_at(offset, sign):
        y = lax.rem(lax.div(c, 4) + sign * offset[0] + ny, ny)
        return y * 2 + lax.rem(lax.rem(lax.div(c, 2), 2) + offset[1], 2)

    def slot_of(offset):
        return (offset[0] * 2 + offset[1]) * 2

    def backward(inst, vector, prepare, first):
        zb[inst, 0] = vector.astype(jnp.bfloat16)
        squares = square_sum(vector) if first else None
        if first:
            tiles[tpd] = jnp.zeros((TILE, TILE), jnp.bfloat16)
            ttiles[tpd] = jnp.zeros((TILE, TILE), jnp.bfloat16)
            pl.semaphore_wait(barrier, len(greeted))
        for dz in reversed(ORDER[nz][1:]):
            send(zb.at[inst, 0], zb.at[inst, dz * nx], zb_send.at[inst], zb_z.at[inst, dz], z_peer(dz))
        for dx in reversed(ORDER[nx][1:]):
            send(zb.at[inst, 0], zb.at[inst, dx], zb_send.at[inst], zb_x.at[inst, 0], x_peer(dx))
        if first:
            norm_start(0, squares, "z")
        else:
            squares = square_sum(vector)
            norm_start(3, squares, "row")
        for piece in range(nc):
            outp[piece] = jnp.zeros((sides, PIECE), jnp.float32)
        if first:
            make_index()
            load.wait()
        for dz in ORDER[nz][1:]:
            take(zb.at[inst, dz * nx], zb_z.at[inst, dz])
            for dx in reversed(ORDER[nx][1:]):
                send(
                    zb.at[inst, dz * nx],
                    zb.at[inst, dz * nx + dx],
                    zb_send.at[inst],
                    zb_x.at[inst, dz],
                    x_peer(dx),
                )
        if first:
            squares = norm_finish(0, squares, "z")
            norm_start(1, squares, "x")

        def add(dz, steps, k):
            origin = lax.rem(zh - dz + nz, nz) * nx
            total = None
            for dx in steps:
                block = origin + lax.rem(x - dx + nx, nx)
                product = dot(zb[inst, dz * nx + dx], tiles[idx_s[0, block * cbg + k]])
                total = product if total is None else total + product
            return total

        def group(i, carry):
            dz = order(i)
            take(zb.at[inst, pl.ds(dz * nx + 1, nx - 1)], zb_x.at[inst, dz])
            for k in range(cbg):
                total = add(dz, range(nx), k)
                outp[2 * k] += total[:, :PIECE]
                outp[2 * k + 1] += total[:, PIECE:]
            return carry

        lax.fori_loop(0, nz - 1, group, 0)
        last = ORDER[nz][-1]
        for k in range(cbg):
            total = add(last, [0], k)
            outp[2 * k] += total[:, :PIECE]
            outp[2 * k + 1] += total[:, PIECE:]
        squares = norm_finish(1, squares, "x") if first else norm_finish(3, squares, "row")
        n = 2 if first else 4
        norm_start(n, squares, "col")
        take(zb.at[inst, pl.ds(last * nx + 1, nx - 1)], zb_x.at[inst, last])
        for some in batches(chips[::-1], BACK_BATCH):
            ready = []
            for offset in some:
                k = chip_at(offset, 1)
                total = add(last, range(1, nx), k)
                for h in range(2):
                    value = outp[2 * k + h] + total[:, h * PIECE : (h + 1) * PIECE]
                    slot = slot_of(offset)
                    if any(offset):
                        csend[inst, slot + h] = value.astype(jnp.bfloat16)
                        ready.append((slot, h, 2 * k + h))
                    else:
                        outp[2 * k + h] = value
            for slot, h, piece in ready:
                send(
                    csend.at[inst, slot + h],
                    crecv.at[inst, slot + core],
                    c_send.at[inst],
                    c_sem.at[inst],
                    (r, piece),
                )
        csend[inst, 0] = outp[c + 1 - 2 * core].astype(jnp.bfloat16)
        send(
            csend.at[inst, 0],
            crecv.at[inst, core],
            c_send.at[inst],
            c_sem.at[inst],
            (r, c + 1 - 2 * core),
        )
        if first:
            make_transposed(0, tpd)
        squares = norm_finish(n, squares, "col")
        norm = jnp.sqrt(to_column(squares) + EPSILON)
        prepared = prepare(norm)
        take(crecv.at[inst, pl.ds(1, nc - 1)], c_sem.at[inst])
        total = outp[c] + crecv[inst, 1 - core].astype(jnp.float32)
        for slot in range(2, nc):
            total = total + crecv[inst, slot].astype(jnp.float32)
        return total, norm, prepared

    def forward(inst, vector, n, prepare):
        wrecv[inst, core] = vector.astype(jnp.bfloat16)
        for offset in reversed(chips):
            slot = slot_of(offset)
            chip = chip_at(offset, 1)
            targets = [2 * chip, 2 * chip + 1] if any(offset) else [c + 1 - 2 * core]
            for target in targets:
                send(
                    wrecv.at[inst, core],
                    wrecv.at[inst, slot + core],
                    w_send.at[inst],
                    w_sem.at[inst, slot // 2],
                    (r, target),
                )
        squares = square_sum(vector)
        norm_start(n, squares, "col")

        def arrive(offset):
            slot = slot_of(offset)
            if any(offset):
                take(wrecv.at[inst, pl.ds(slot, 2)], w_sem.at[inst, slot // 2])
            else:
                take(wrecv.at[inst, pl.ds(1 - core, 1)], w_sem.at[inst, 0])
            wfull[slot // 2, :, :PIECE] = wrecv[inst, slot]
            wfull[slot // 2, :, PIECE:] = wrecv[inst, slot + 1]

        def add(block, offsets):
            total = None
            for offset in offsets:
                k = chip_at(offset, -1)
                product = dot(wfull[slot_of(offset) // 2], ttiles[idx_s[0, block * cbg + k]])
                total = product if total is None else total + product
            return total

        def block_at(dz, dx):
            return lax.rem(zh + dz, nz) * nx + lax.rem(x + dx, nx)

        stages = [chips[s : s + 2] for s in range(0, len(chips), 2)]
        for s, offsets in enumerate(stages[:-1]):
            for offset in offsets:
                arrive(offset)
            for slot in range(nr):
                total = add(block_at(slot // nx, slot % nx), offsets)
                part[slot] = total if s == 0 else part[slot] + total
        squares = norm_finish(n, squares, "col")
        norm_start(n + 1, squares, "row")
        for offset in stages[-1]:
            arrive(offset)
        slots = [dz * nx + dx for dz in reversed(ORDER[nz]) for dx in reversed(ORDER[nx])]
        for some in batches(slots, FORWARD_BATCH):
            for slot in some:
                total = add(block_at(slot // nx, slot % nx), stages[-1])
                if len(stages) > 1:
                    total = part[slot] + total
                if slot % nx == 0:
                    part[slot] = total
                else:
                    s1send[inst, slot] = total.astype(jnp.bfloat16)
            for slot in some:
                if slot % nx:
                    send(
                        s1send.at[inst, slot],
                        s1recv.at[inst, slot],
                        s1_send.at[inst],
                        s1_sem.at[inst, slot // nx],
                        x_peer(slot % nx),
                    )
        total = None
        for dz in reversed(ORDER[nz]):
            take(s1recv.at[inst, pl.ds(dz * nx + 1, nx - 1)], s1_sem.at[inst, dz])
            total = part[dz * nx]
            for dx in range(1, nx):
                total = total + s1recv[inst, dz * nx + dx].astype(jnp.float32)
            if dz:
                s2send[inst, dz] = total.astype(jnp.bfloat16)
                send(
                    s2send.at[inst, dz],
                    s2recv.at[inst, dz],
                    s2_send.at[inst],
                    s2_sem.at[inst],
                    z_peer(dz),
                )
        squares = norm_finish(n + 1, squares, "row")
        norm = jnp.sqrt(to_column(squares) + EPSILON)
        prepared = prepare(norm)
        take(s2recv.at[inst, pl.ds(1, nz - 1)], s2_sem.at[inst])
        for dz in range(1, nz):
            total = total + s2recv[inst, dz].astype(jnp.float32)
        return total, norm, prepared

    for copy in small:
        copy.wait()
    back, beta0, scale = backward(0, rhs[...], lambda norm: 1.0 / norm, True)
    right_raw0 = back * scale
    forward1, alpha0, (scale, shift) = forward(
        0, right_raw0, 5, lambda norm: (1.0 / norm, (norm / beta0) * rhs[...])
    )
    left_raw1 = forward1 * scale - shift
    first_f[...] = forward1
    back, beta1, (scale, shift) = backward(
        1, left_raw1, lambda norm: (1.0 / norm, (norm / alpha0) * right_raw0), False
    )
    right_raw1 = back * scale - shift
    forward2, alpha1, (scale, shift) = forward(
        1, right_raw1, 7, lambda norm: (1.0 / norm, (norm / beta1) * left_raw1)
    )
    left_raw2 = forward2 * scale - shift

    squares = square_sum(left_raw2)
    norm_start(9, squares, "core")
    squares = norm_finish(9, squares, "core")
    norm_start(10, squares, "chips")
    rho_bar = alpha0
    phi_bar = beta0
    rho_value = jnp.sqrt(rho_bar * rho_bar + beta1 * beta1)
    cosine = rho_bar / rho_value
    sine_value = beta1 / rho_value
    theta_value = sine_value * alpha1
    step0 = cosine * phi_bar / rho_value
    turn0 = theta_value / rho_value
    rho_bar = -cosine * alpha1
    phi_bar = sine_value * phi_bar
    squares = norm_finish(10, squares, "chips")
    beta2 = jnp.sqrt(to_column(squares) + EPSILON)
    rho_value = jnp.sqrt(rho_bar * rho_bar + beta2 * beta2)
    step1 = rho_bar / rho_value * phi_bar / rho_value
    weight0 = step0 - step1 * turn0
    weight0 = weight0 / alpha0
    weight1 = step1 / alpha1
    sol_out[...] = weight0 * right_raw0 + weight1 * right_raw1
    res_out[...] = rhs[...] - weight0 * first_f[...] - weight1 * forward2

    for inst in range(2):
        take(zb.at[inst, pl.ds(1, nr - 1)], zb_send.at[inst])
        take(s1recv.at[inst, pl.ds(0, nz * (nx - 1))], s1_send.at[inst])
        take(s2recv.at[inst, pl.ds(1, nz - 1)], s2_send.at[inst])
        take(crecv.at[inst, pl.ds(1, nc - 1)], c_send.at[inst])
        take(wrecv.at[inst, pl.ds(1, nc - 1)], w_send.at[inst])
    kinds = ("z", "x", "col", "row", "col", "col", "row", "col", "row", "core")
    for n, kind in enumerate(kinds):
        take(nrecv.at[n, pl.ds(0, len(peers[kind]))], n_send.at[n])
    take(frecv.at[pl.ds(0, len(peers["chips"]))], n_send.at[10])


def place(solution, residual, sol_out, res_out):
    sol_out[:, 0, :] = solution[...]
    res_out[:, 0, :] = residual[...]


def local(dims, right_side, tile_values, tile_rows, tile_cols, tile_count):
    nz, nx, nc, cbg, tpd, sides = dims
    nr = nz * nx
    bf16, f32, i32 = jnp.bfloat16, jnp.float32, jnp.int32
    vmem = pl.BlockSpec(memory_space=pltpu.VMEM)
    dma = pltpu.SemaphoreType.DMA
    solution, residual = pl.pallas_call(
        functools.partial(kernel, dims),
        out_shape=(
            jax.ShapeDtypeStruct((sides, PIECE), f32),
            jax.ShapeDtypeStruct((sides, TILE), f32),
        ),
        in_specs=[pl.BlockSpec(memory_space=pltpu.HBM)] * 5,
        out_specs=(vmem, vmem),
        scratch_shapes=[
            pltpu.SMEM((1, 1, tpd), i32),
            pltpu.SMEM((1, 1, tpd), i32),
            pltpu.SMEM((1, 1), i32),
            pltpu.VMEM((sides, TILE), f32),
            pltpu.VMEM((tpd + 1, TILE, TILE), bf16),
            pltpu.VMEM((tpd + 1, TILE, TILE), bf16),
            pltpu.VMEM((8, 128), i32),
            pltpu.SMEM((8, 128), i32),
            pltpu.VMEM((2, nr, sides, TILE), bf16),
            pltpu.VMEM((2, nr, sides, TILE), bf16),
            pltpu.VMEM((2, nr, sides, TILE), bf16),
            pltpu.VMEM((2, nz, sides, TILE), bf16),
            pltpu.VMEM((2, nz, sides, TILE), bf16),
            pltpu.VMEM((nr, sides, TILE), f32),
            pltpu.VMEM((2, nc, sides, PIECE), bf16),
            pltpu.VMEM((2, nc, sides, PIECE), bf16),
            pltpu.VMEM((2, nc, sides, PIECE), bf16),
            pltpu.VMEM((cbg, sides, TILE), bf16),
            pltpu.VMEM((nc, sides, PIECE), f32),
            pltpu.VMEM((sides, TILE), f32),
            pltpu.VMEM((16, 128), f32),
            pltpu.VMEM((10, max(nr, nc), 128), f32),
            pltpu.VMEM((nr * nc // 2, 128), f32),
            dma,
            dma((3,)),
            dma,
            dma,
            dma((2,)),
            dma((2, nz)),
            dma((2, nz)),
            dma((2,)),
            dma((2, nz)),
            dma((2,)),
            dma((2,)),
            dma((2,)),
            dma((2,)),
            dma((2,)),
            dma((2, cbg)),
            dma((11,)),
            dma((11,)),
        ],
        compiler_params=pltpu.CompilerParams(
            collective_id=0, has_side_effects=True, vmem_limit_bytes=62 * 2**20
        ),
        name="lsqr",
    )(tile_rows, tile_cols, tile_count, right_side, tile_values)
    return pl.pallas_call(
        place,
        out_shape=(
            jax.ShapeDtypeStruct((sides, 1, PIECE), f32),
            jax.ShapeDtypeStruct((sides, 1, TILE), f32),
        ),
        in_specs=[vmem, vmem],
        out_specs=(vmem, vmem),
        name="place",
    )(solution, residual)


def solution(mesh):
    in_specs = (
        P(None, "col", "row"),
        P("row", "col", None, None, None),
        P("row", "col", None),
        P("row", "col", None),
        P("row", "col"),
    )
    out_specs = (P(None, "row", "col"), P(None, "col", "row"))
    nr, nc = mesh.shape["row"], mesh.shape["col"]
    nz = 4 if nr == 16 else 2

    def program(right_side, tile_values, tile_rows, tile_cols, tile_count):
        dims = (nz, nr // nz, nc, nc * PIECE // TILE, tile_values.shape[2], right_side.shape[0])
        return jax.shard_map(
            functools.partial(local, dims),
            mesh=mesh,
            in_specs=in_specs,
            out_specs=out_specs,
            check_vma=False,
        )(right_side, tile_values, tile_rows, tile_cols, tile_count)

    return program
```

```python
import functools
import itertools

import jax
import jax.numpy as jnp
from jax import lax
from jax.experimental import pallas as pl
from jax.experimental.pallas import tpu as pltpu
from jax.sharding import PartitionSpec as P

MESH = pl.DeviceIdType.MESH
EPSILON = 1e-06
TILE = 256
PIECE = 128
BACK_BATCH = 2
FORWARD_BATCH = 2


def order(i):
    return i + lax.div(i, 2) - 2 * lax.div(i, 3)


ORDER = {2: (0, 1), 4: (0, 1, 3, 2)}


def batches(items, size):
    return [items[i : i + size] for i in range(0, len(items), size)]


def dot(a, b):
    return jnp.dot(a, b, preferred_element_type=jnp.float32)


def kernel(
    dims,
    rows_hbm,
    cols_hbm,
    count_hbm,
    rhs_hbm,
    tiles_hbm,
    sol_out,
    res_out,
    rows_s,
    cols_s,
    count_s,
    rhs,
    tiles,
    ttiles,
    idx_v,
    idx_s,
    zb,
    s1send,
    s1recv,
    s2send,
    s2recv,
    part,
    csend,
    crecv,
    wrecv,
    wfull,
    outp,
    first_f,
    nsend,
    nrecv,
    frecv,
    tile_sem,
    small_sem,
    rhs_sem,
    idx_sem,
    zb_send,
    zb_z,
    zb_x,
    s1_send,
    s1_sem,
    s2_send,
    s2_sem,
    c_send,
    c_sem,
    w_send,
    w_sem,
    n_send,
    n_sem,
):
    nz, nx, nc, cbg, tpd, sides = dims
    nr = nz * nx
    ny = nc // 4
    r = lax.axis_index("row")
    c = lax.axis_index("col")
    zh = lax.div(r, nx)
    x = lax.rem(r, nx)

    load = pltpu.make_async_copy(tiles_hbm.at[0, 0], tiles.at[pl.ds(0, tpd)], tile_sem)
    small = [
        pltpu.make_async_copy(rows_hbm, rows_s, small_sem.at[0]),
        pltpu.make_async_copy(cols_hbm, cols_s, small_sem.at[1]),
        pltpu.make_async_copy(count_hbm, count_s, small_sem.at[2]),
        pltpu.make_async_copy(rhs_hbm.at[:, 0, :], rhs, rhs_sem),
    ]
    for copy in small:
        copy.start()

    load.start()

    barrier = pltpu.get_barrier_semaphore()

    def x_peer(dx):
        return (zh * nx + lax.rem(x + dx, nx), c)

    def z_peer(dz):
        return (lax.rem(zh + dz, nz) * nx + x, c)

    def at_offset(offset, dc):
        z = lax.rem(2 * zh + lax.rem(lax.div(c, 2), 2) + offset[0], 2 * nz)
        y = lax.rem(lax.div(c, 4) + offset[2], ny)
        core = lax.rem(lax.rem(c, 2) + dc, 2)
        return (
            lax.div(z, 2) * nx + lax.rem(x + offset[1], nx),
            y * 4 + lax.rem(z, 2) * 2 + core,
        )

    sizes = (2 * nz, nx, ny)
    offsets = sorted(
        itertools.product(*map(range, sizes)),
        key=lambda o: -sum(min(d, s - d) for d, s in zip(o, sizes)),
    )
    peers = {
        "x": [x_peer(dx) for dx in range(1, nx)],
        "z": [z_peer(dz) for dz in range(1, nz)],
        "row": [(lax.rem(r + d, nr), c) for d in range(1, nr)],
        "col": [(r, lax.rem(c + d, nc)) for d in range(1, nc)],
        "core": [at_offset((0, 0, 0), 1)],
        "chips": [at_offset(o, 0) for o in offsets if any(o)],
    }
    greeted = peers["z"] + peers["x"] + peers["col"]
    for device in greeted:
        pl.semaphore_signal(barrier, inc=1, device_id=device, device_id_type=MESH)

    def send(src, dst, send_sem, recv_sem, device):
        pltpu.make_async_remote_copy(
            src_ref=src,
            dst_ref=dst,
            send_sem=send_sem,
            recv_sem=recv_sem,
            device_id=device,
            device_id_type=MESH,
        ).start()

    def take(ref, sem):
        pltpu.make_async_copy(ref, ref, sem).wait()

    eye = (
        lax.broadcasted_iota(jnp.int32, (sides, 128), 0)
        == lax.broadcasted_iota(jnp.int32, (sides, 128), 1)
    ).astype(jnp.float32)

    def to_row(column):
        return jnp.sum(column * eye, axis=0, keepdims=True)

    def to_column(row):
        return jnp.sum(row * eye, axis=1, keepdims=True)

    def square_sum(array):
        return to_row(jnp.sum(array * array, axis=1, keepdims=True))

    def norm_start(n, value, kind):
        nsend[pl.ds(n, 1), :] = value
        slots = frecv if kind == "chips" else nrecv.at[n]
        for d, device in enumerate(peers[kind]):
            send(nsend.at[pl.ds(n, 1)], slots.at[pl.ds(d, 1)], n_send.at[n], n_sem.at[n], device)

    def norm_finish(n, value, kind):
        slots = frecv if kind == "chips" else nrecv.at[n]
        size = len(peers[kind])
        take(slots.at[pl.ds(0, size)], n_sem.at[n])
        return value + jnp.sum(slots[0:size, :], axis=0, keepdims=True)

    def make_index():
        lane = lax.broadcasted_iota(jnp.int32, (8, 128), 1)
        count = count_s[0, 0]

        def one(t, table):
            key = rows_s[0, 0, t] * cbg + cols_s[0, 0, t]
            key = jnp.where(t < count, key, -1)
            return jnp.where(lane == key, t, table)

        idx_v[...] = lax.fori_loop(0, tpd, one, jnp.full((8, 128), tpd, jnp.int32))
        copy = pltpu.make_async_copy(idx_v, idx_s, idx_sem)
        copy.start()
        copy.wait()

    def make_transposed(begin, end):
        def some(step, carry):
            for u in range(4):
                ttiles[step * 4 + u] = tiles[step * 4 + u].T
            return carry

        lax.fori_loop(begin // 4, end // 4, some, 0)

    chips = sorted(
        itertools.product(range(ny), range(2)), key=lambda o: (min(o[0], ny - o[0]), o[1])
    )
    core = lax.rem(c, 2)

    def chip_at(offset, sign):
        y = lax.rem(lax.div(c, 4) + sign * offset[0] + ny, ny)
        return y * 2 + lax.rem(lax.rem(lax.div(c, 2), 2) + offset[1], 2)

    def slot_of(offset):
        return (offset[0] * 2 + offset[1]) * 2

    def backward(inst, vector, prepare, first):
        zb[inst, 0] = vector.astype(jnp.bfloat16)
        squares = square_sum(vector) if first else None
        if first:
            tiles[tpd] = jnp.zeros((TILE, TILE), jnp.bfloat16)
            ttiles[tpd] = jnp.zeros((TILE, TILE), jnp.bfloat16)
            pl.semaphore_wait(barrier, len(greeted))
        for dz in reversed(ORDER[nz][1:]):
            send(zb.at[inst, 0], zb.at[inst, dz * nx], zb_send.at[inst], zb_z.at[inst, dz], z_peer(dz))
        for dx in reversed(ORDER[nx][1:]):
            send(zb.at[inst, 0], zb.at[inst, dx], zb_send.at[inst], zb_x.at[inst, 0], x_peer(dx))
        if first:
            norm_start(0, squares, "z")
        else:
            squares = square_sum(vector)
            norm_start(3, squares, "row")
        for piece in range(nc):
            outp[piece] = jnp.zeros((sides, PIECE), jnp.float32)
        if first:
            make_index()
            load.wait()
        for dz in ORDER[nz][1:]:
            take(zb.at[inst, dz * nx], zb_z.at[inst, dz])
            for dx in reversed(ORDER[nx][1:]):
                send(
                    zb.at[inst, dz * nx],
                    zb.at[inst, dz * nx + dx],
                    zb_send.at[inst],
                    zb_x.at[inst, dz],
                    x_peer(dx),
                )
        if first:
            squares = norm_finish(0, squares, "z")
            norm_start(1, squares, "x")

        def add(dz, steps, k):
            origin = lax.rem(zh - dz + nz, nz) * nx
            total = None
            for dx in steps:
                block = origin + lax.rem(x - dx + nx, nx)
                product = dot(zb[inst, dz * nx + dx], tiles[idx_s[0, block * cbg + k]])
                total = product if total is None else total + product
            return total

        def group(i, carry):
            dz = order(i)
            take(zb.at[inst, pl.ds(dz * nx + 1, nx - 1)], zb_x.at[inst, dz])
            for k in range(cbg):
                total = add(dz, range(nx), k)
                outp[2 * k] += total[:, :PIECE]
                outp[2 * k + 1] += total[:, PIECE:]
            return carry

        lax.fori_loop(0, nz - 1, group, 0)
        last = ORDER[nz][-1]
        for k in range(cbg):
            total = add(last, [0], k)
            outp[2 * k] += total[:, :PIECE]
            outp[2 * k + 1] += total[:, PIECE:]
        squares = norm_finish(1, squares, "x") if first else norm_finish(3, squares, "row")
        n = 2 if first else 4
        norm_start(n, squares, "col")
        take(zb.at[inst, pl.ds(last * nx + 1, nx - 1)], zb_x.at[inst, last])
        for some in batches(chips[::-1], BACK_BATCH):
            ready = []
            for offset in some:
                k = chip_at(offset, 1)
                total = add(last, range(1, nx), k)
                for h in range(2):
                    value = outp[2 * k + h] + total[:, h * PIECE : (h + 1) * PIECE]
                    slot = slot_of(offset)
                    if any(offset):
                        csend[inst, slot + h] = value.astype(jnp.bfloat16)
                        ready.append((slot, h, 2 * k + h))
                    else:
                        outp[2 * k + h] = value
            for slot, h, piece in ready:
                send(
                    csend.at[inst, slot + h],
                    crecv.at[inst, slot + core],
                    c_send.at[inst],
                    c_sem.at[inst],
                    (r, piece),
                )
        csend[inst, 0] = outp[c + 1 - 2 * core].astype(jnp.bfloat16)
        send(
            csend.at[inst, 0],
            crecv.at[inst, core],
            c_send.at[inst],
            c_sem.at[inst],
            (r, c + 1 - 2 * core),
        )
        if first:
            make_transposed(0, tpd)
        squares = norm_finish(n, squares, "col")
        norm = jnp.sqrt(to_column(squares) + EPSILON)
        prepared = prepare(norm)
        take(crecv.at[inst, pl.ds(1, nc - 1)], c_sem.at[inst])
        total = outp[c] + crecv[inst, 1 - core].astype(jnp.float32)
        for slot in range(2, nc):
            total = total + crecv[inst, slot].astype(jnp.float32)
        return total, norm, prepared

    def forward(inst, vector, n, prepare):
        wrecv[inst, core] = vector.astype(jnp.bfloat16)
        for offset in reversed(chips):
            slot = slot_of(offset)
            chip = chip_at(offset, 1)
            targets = [2 * chip, 2 * chip + 1] if any(offset) else [c + 1 - 2 * core]
            for target in targets:
                send(
                    wrecv.at[inst, core],
                    wrecv.at[inst, slot + core],
                    w_send.at[inst],
                    w_sem.at[inst, slot // 2],
                    (r, target),
                )
        squares = square_sum(vector)
        norm_start(n, squares, "col")

        def arrive(offset):
            slot = slot_of(offset)
            if any(offset):
                take(wrecv.at[inst, pl.ds(slot, 2)], w_sem.at[inst, slot // 2])
            else:
                take(wrecv.at[inst, pl.ds(1 - core, 1)], w_sem.at[inst, 0])
            wfull[slot // 2, :, :PIECE] = wrecv[inst, slot]
            wfull[slot // 2, :, PIECE:] = wrecv[inst, slot + 1]

        def add(block):
            total = None
            for offset in chips:
                k = chip_at(offset, -1)
                product = dot(wfull[slot_of(offset) // 2], ttiles[idx_s[0, block * cbg + k]])
                total = product if total is None else total + product
            return total

        def block_at(dz, dx):
            return lax.rem(zh + dz, nz) * nx + lax.rem(x + dx, nx)

        for offset in chips:
            arrive(offset)
        slots = [dz * nx + dx for dz in reversed(ORDER[nz]) for dx in reversed(ORDER[nx])]
        for some in batches(slots, FORWARD_BATCH):
            for slot in some:
                total = add(block_at(slot // nx, slot % nx))
                if slot % nx == 0:
                    part[slot // nx] = total
                else:
                    s1send[inst, slot] = total.astype(jnp.bfloat16)
            for slot in some:
                if slot % nx:
                    send(
                        s1send.at[inst, slot],
                        s1recv.at[inst, slot],
                        s1_send.at[inst],
                        s1_sem.at[inst, slot // nx],
                        x_peer(slot % nx),
                    )
        squares = norm_finish(n, squares, "col")
        norm_start(n + 1, squares, "row")
        total = None
        for dz in reversed(ORDER[nz]):
            take(s1recv.at[inst, pl.ds(dz * nx + 1, nx - 1)], s1_sem.at[inst, dz])
            total = part[dz]
            for dx in range(1, nx):
                total = total + s1recv[inst, dz * nx + dx].astype(jnp.float32)
            if dz:
                s2send[inst, dz] = total.astype(jnp.bfloat16)
                send(
                    s2send.at[inst, dz],
                    s2recv.at[inst, dz],
                    s2_send.at[inst],
                    s2_sem.at[inst],
                    z_peer(dz),
                )
        squares = norm_finish(n + 1, squares, "row")
        norm = jnp.sqrt(to_column(squares) + EPSILON)
        prepared = prepare(norm)
        take(s2recv.at[inst, pl.ds(1, nz - 1)], s2_sem.at[inst])
        for dz in range(1, nz):
            total = total + s2recv[inst, dz].astype(jnp.float32)
        return total, norm, prepared

    for copy in small:
        copy.wait()
    back, beta0, scale = backward(0, rhs[...], lambda norm: 1.0 / norm, True)
    right_raw0 = back * scale
    forward1, alpha0, (scale, shift) = forward(
        0, right_raw0, 5, lambda norm: (1.0 / norm, (norm / beta0) * rhs[...])
    )
    left_raw1 = forward1 * scale - shift
    first_f[...] = forward1
    back, beta1, (scale, shift) = backward(
        1, left_raw1, lambda norm: (1.0 / norm, (norm / alpha0) * right_raw0), False
    )
    right_raw1 = back * scale - shift
    forward2, alpha1, (scale, shift) = forward(
        1, right_raw1, 7, lambda norm: (1.0 / norm, (norm / beta1) * left_raw1)
    )
    left_raw2 = forward2 * scale - shift

    squares = square_sum(left_raw2)
    norm_start(9, squares, "core")
    squares = norm_finish(9, squares, "core")
    norm_start(10, squares, "chips")
    rho_bar = alpha0
    phi_bar = beta0
    rho_value = jnp.sqrt(rho_bar * rho_bar + beta1 * beta1)
    cosine = rho_bar / rho_value
    sine_value = beta1 / rho_value
    theta_value = sine_value * alpha1
    step0 = cosine * phi_bar / rho_value
    turn0 = theta_value / rho_value
    rho_bar = -cosine * alpha1
    phi_bar = sine_value * phi_bar
    squares = norm_finish(10, squares, "chips")
    beta2 = jnp.sqrt(to_column(squares) + EPSILON)
    rho_value = jnp.sqrt(rho_bar * rho_bar + beta2 * beta2)
    step1 = rho_bar / rho_value * phi_bar / rho_value
    weight0 = step0 - step1 * turn0
    weight0 = weight0 / alpha0
    weight1 = step1 / alpha1
    sol_out[...] = weight0 * right_raw0 + weight1 * right_raw1
    res_out[...] = rhs[...] - weight0 * first_f[...] - weight1 * forward2

    for inst in range(2):
        take(zb.at[inst, pl.ds(1, nr - 1)], zb_send.at[inst])
        take(s1recv.at[inst, pl.ds(0, nz * (nx - 1))], s1_send.at[inst])
        take(s2recv.at[inst, pl.ds(1, nz - 1)], s2_send.at[inst])
        take(crecv.at[inst, pl.ds(1, nc - 1)], c_send.at[inst])
        take(wrecv.at[inst, pl.ds(1, nc - 1)], w_send.at[inst])
    kinds = ("z", "x", "col", "row", "col", "col", "row", "col", "row", "core")
    for n, kind in enumerate(kinds):
        take(nrecv.at[n, pl.ds(0, len(peers[kind]))], n_send.at[n])
    take(frecv.at[pl.ds(0, len(peers["chips"]))], n_send.at[10])


def place(solution, residual, sol_out, res_out):
    sol_out[:, 0, :] = solution[...]
    res_out[:, 0, :] = residual[...]


def local(dims, right_side, tile_values, tile_rows, tile_cols, tile_count):
    nz, nx, nc, cbg, tpd, sides = dims
    nr = nz * nx
    bf16, f32, i32 = jnp.bfloat16, jnp.float32, jnp.int32
    vmem = pl.BlockSpec(memory_space=pltpu.VMEM)
    dma = pltpu.SemaphoreType.DMA
    solution, residual = pl.pallas_call(
        functools.partial(kernel, dims),
        out_shape=(
            jax.ShapeDtypeStruct((sides, PIECE), f32),
            jax.ShapeDtypeStruct((sides, TILE), f32),
        ),
        in_specs=[pl.BlockSpec(memory_space=pltpu.HBM)] * 5,
        out_specs=(vmem, vmem),
        scratch_shapes=[
            pltpu.SMEM((1, 1, tpd), i32),
            pltpu.SMEM((1, 1, tpd), i32),
            pltpu.SMEM((1, 1), i32),
            pltpu.VMEM((sides, TILE), f32),
            pltpu.VMEM((tpd + 1, TILE, TILE), bf16),
            pltpu.VMEM((tpd + 1, TILE, TILE), bf16),
            pltpu.VMEM((8, 128), i32),
            pltpu.SMEM((8, 128), i32),
            pltpu.VMEM((2, nr, sides, TILE), bf16),
            pltpu.VMEM((2, nr, sides, TILE), bf16),
            pltpu.VMEM((2, nr, sides, TILE), bf16),
            pltpu.VMEM((2, nz, sides, TILE), bf16),
            pltpu.VMEM((2, nz, sides, TILE), bf16),
            pltpu.VMEM((nz, sides, TILE), f32),
            pltpu.VMEM((2, nc, sides, PIECE), bf16),
            pltpu.VMEM((2, nc, sides, PIECE), bf16),
            pltpu.VMEM((2, nc, sides, PIECE), bf16),
            pltpu.VMEM((cbg, sides, TILE), bf16),
            pltpu.VMEM((nc, sides, PIECE), f32),
            pltpu.VMEM((sides, TILE), f32),
            pltpu.VMEM((16, 128), f32),
            pltpu.VMEM((10, max(nr, nc), 128), f32),
            pltpu.VMEM((nr * nc // 2, 128), f32),
            dma,
            dma((3,)),
            dma,
            dma,
            dma((2,)),
            dma((2, nz)),
            dma((2, nz)),
            dma((2,)),
            dma((2, nz)),
            dma((2,)),
            dma((2,)),
            dma((2,)),
            dma((2,)),
            dma((2,)),
            dma((2, cbg)),
            dma((11,)),
            dma((11,)),
        ],
        compiler_params=pltpu.CompilerParams(
            collective_id=0, has_side_effects=True, vmem_limit_bytes=62 * 2**20
        ),
        name="lsqr",
    )(tile_rows, tile_cols, tile_count, right_side, tile_values)
    return pl.pallas_call(
        place,
        out_shape=(
            jax.ShapeDtypeStruct((sides, 1, PIECE), f32),
            jax.ShapeDtypeStruct((sides, 1, TILE), f32),
        ),
        in_specs=[vmem, vmem],
        out_specs=(vmem, vmem),
        name="place",
    )(solution, residual)


def solution(mesh):
    in_specs = (
        P(None, "col", "row"),
        P("row", "col", None, None, None),
        P("row", "col", None),
        P("row", "col", None),
        P("row", "col"),
    )
    out_specs = (P(None, "row", "col"), P(None, "col", "row"))
    nr, nc = mesh.shape["row"], mesh.shape["col"]
    nz = 4 if nr == 16 else 2

    def program(right_side, tile_values, tile_rows, tile_cols, tile_count):
        dims = (nz, nr // nz, nc, nc * PIECE // TILE, tile_values.shape[2], right_side.shape[0])
        return jax.shard_map(
            functools.partial(local, dims),
            mesh=mesh,
            in_specs=in_specs,
            out_specs=out_specs,
            check_vma=False,
        )(right_side, tile_values, tile_rows, tile_cols, tile_count)

    return program
```

```python
import functools
import itertools

import jax
import jax.numpy as jnp
from jax import lax
from jax.experimental import pallas as pl
from jax.experimental.pallas import tpu as pltpu
from jax.sharding import PartitionSpec as P

MESH = pl.DeviceIdType.MESH
EPSILON = 1e-06
TILE = 256
PIECE = 128
BACK_BATCH = 2
FORWARD_BATCH = 2


def order(i):
    return i + lax.div(i, 2) - 2 * lax.div(i, 3)


ORDER = {2: (0, 1), 4: (0, 1, 3, 2)}


def batches(items, size):
    return [items[i : i + size] for i in range(0, len(items), size)]


def dot(a, b):
    return jnp.dot(a, b, preferred_element_type=jnp.float32)


def kernel(
    dims,
    rows_hbm,
    cols_hbm,
    count_hbm,
    rhs_hbm,
    tiles_hbm,
    sol_out,
    res_out,
    rows_s,
    cols_s,
    count_s,
    rhs,
    tiles,
    ttiles,
    idx_v,
    idx_s,
    zb,
    s1send,
    s1recv,
    s2send,
    s2recv,
    part,
    csend,
    crecv,
    wrecv,
    wfull,
    outp,
    first_f,
    nsend,
    nrecv,
    frecv,
    tile_sem,
    small_sem,
    rhs_sem,
    idx_sem,
    zb_send,
    zb_z,
    zb_x,
    s1_send,
    s1_sem,
    s2_send,
    s2_sem,
    c_send,
    c_sem,
    w_send,
    w_sem,
    n_send,
    n_sem,
):
    nz, nx, nc, cbg, tpd, sides = dims
    nr = nz * nx
    ny = nc // 4
    r = lax.axis_index("row")
    c = lax.axis_index("col")
    zh = lax.div(r, nx)
    x = lax.rem(r, nx)

    load = pltpu.make_async_copy(tiles_hbm.at[0, 0], tiles.at[pl.ds(0, tpd)], tile_sem)
    small = [
        pltpu.make_async_copy(rows_hbm, rows_s, small_sem.at[0]),
        pltpu.make_async_copy(cols_hbm, cols_s, small_sem.at[1]),
        pltpu.make_async_copy(count_hbm, count_s, small_sem.at[2]),
        pltpu.make_async_copy(rhs_hbm.at[:, 0, :], rhs, rhs_sem),
    ]
    for copy in small:
        copy.start()

    load.start()

    barrier = pltpu.get_barrier_semaphore()

    def x_peer(dx):
        return (zh * nx + lax.rem(x + dx, nx), c)

    def z_peer(dz):
        return (lax.rem(zh + dz, nz) * nx + x, c)

    def at_offset(offset, dc):
        z = lax.rem(2 * zh + lax.rem(lax.div(c, 2), 2) + offset[0], 2 * nz)
        y = lax.rem(lax.div(c, 4) + offset[2], ny)
        core = lax.rem(lax.rem(c, 2) + dc, 2)
        return (
            lax.div(z, 2) * nx + lax.rem(x + offset[1], nx),
            y * 4 + lax.rem(z, 2) * 2 + core,
        )

    sizes = (2 * nz, nx, ny)
    offsets = sorted(
        itertools.product(*map(range, sizes)),
        key=lambda o: -sum(min(d, s - d) for d, s in zip(o, sizes)),
    )
    peers = {
        "x": [x_peer(dx) for dx in range(1, nx)],
        "z": [z_peer(dz) for dz in range(1, nz)],
        "row": [(lax.rem(r + d, nr), c) for d in range(1, nr)],
        "col": [(r, lax.rem(c + d, nc)) for d in range(1, nc)],
        "core": [at_offset((0, 0, 0), 1)],
        "chips": [at_offset(o, 0) for o in offsets if any(o)],
    }
    greeted = peers["z"] + peers["x"] + peers["col"]
    for device in greeted:
        pl.semaphore_signal(barrier, inc=1, device_id=device, device_id_type=MESH)

    def send(src, dst, send_sem, recv_sem, device):
        pltpu.make_async_remote_copy(
            src_ref=src,
            dst_ref=dst,
            send_sem=send_sem,
            recv_sem=recv_sem,
            device_id=device,
            device_id_type=MESH,
        ).start()

    def take(ref, sem):
        pltpu.make_async_copy(ref, ref, sem).wait()

    eye = (
        lax.broadcasted_iota(jnp.int32, (sides, 128), 0)
        == lax.broadcasted_iota(jnp.int32, (sides, 128), 1)
    ).astype(jnp.float32)

    def to_row(column):
        return jnp.sum(column * eye, axis=0, keepdims=True)

    def to_column(row):
        return jnp.sum(row * eye, axis=1, keepdims=True)

    def square_sum(array):
        return to_row(jnp.sum(array * array, axis=1, keepdims=True))

    def norm_start(n, value, kind):
        nsend[pl.ds(n, 1), :] = value
        slots = frecv if kind == "chips" else nrecv.at[n]
        for d, device in enumerate(peers[kind]):
            send(nsend.at[pl.ds(n, 1)], slots.at[pl.ds(d, 1)], n_send.at[n], n_sem.at[n], device)

    def norm_finish(n, value, kind):
        slots = frecv if kind == "chips" else nrecv.at[n]
        size = len(peers[kind])
        take(slots.at[pl.ds(0, size)], n_sem.at[n])
        return value + jnp.sum(slots[0:size, :], axis=0, keepdims=True)

    def make_index():
        lane = lax.broadcasted_iota(jnp.int32, (8, 128), 1)
        count = count_s[0, 0]

        def one(t, table):
            key = rows_s[0, 0, t] * cbg + cols_s[0, 0, t]
            key = jnp.where(t < count, key, -1)
            return jnp.where(lane == key, t, table)

        idx_v[...] = lax.fori_loop(0, tpd, one, jnp.full((8, 128), tpd, jnp.int32))
        copy = pltpu.make_async_copy(idx_v, idx_s, idx_sem)
        copy.start()
        copy.wait()

    def make_transposed(begin, end):
        def some(step, carry):
            for u in range(4):
                ttiles[step * 4 + u] = tiles[step * 4 + u].T
            return carry

        lax.fori_loop(begin // 4, end // 4, some, 0)

    chips = sorted(
        itertools.product(range(ny), range(2)), key=lambda o: (min(o[0], ny - o[0]), o[1])
    )
    core = lax.rem(c, 2)

    def chip_at(offset, sign):
        y = lax.rem(lax.div(c, 4) + sign * offset[0] + ny, ny)
        return y * 2 + lax.rem(lax.rem(lax.div(c, 2), 2) + offset[1], 2)

    def slot_of(offset):
        return (offset[0] * 2 + offset[1]) * 2

    def backward(inst, vector, prepare, first):
        zb[inst, 0] = vector.astype(jnp.bfloat16)
        squares = square_sum(vector) if first else None
        if first:
            tiles[tpd] = jnp.zeros((TILE, TILE), jnp.bfloat16)
            ttiles[tpd] = jnp.zeros((TILE, TILE), jnp.bfloat16)
            pl.semaphore_wait(barrier, len(greeted))
        halves = [pl.ds(h * (sides // 2), sides // 2) for h in range(2)]
        for h, rows in enumerate(halves):
            for dz in reversed(ORDER[nz][1:]):
                send(
                    zb.at[inst, 0, rows],
                    zb.at[inst, dz * nx, rows],
                    zb_send.at[inst],
                    zb_z.at[inst, dz, h],
                    z_peer(dz),
                )
        for dx in reversed(ORDER[nx][1:]):
            send(zb.at[inst, 0], zb.at[inst, dx], zb_send.at[inst], zb_x.at[inst, 0], x_peer(dx))
        if first:
            norm_start(0, squares, "z")
        else:
            squares = square_sum(vector)
            norm_start(3, squares, "row")
        for piece in range(nc):
            outp[piece] = jnp.zeros((sides, PIECE), jnp.float32)
        if first:
            make_index()
            load.wait()
        for dz in ORDER[nz][1:]:
            for h, rows in enumerate(halves):
                take(zb.at[inst, dz * nx, rows], zb_z.at[inst, dz, h])
                for dx in reversed(ORDER[nx][1:]):
                    send(
                        zb.at[inst, dz * nx, rows],
                        zb.at[inst, dz * nx + dx, rows],
                        zb_send.at[inst],
                        zb_x.at[inst, dz],
                        x_peer(dx),
                    )
        if first:
            squares = norm_finish(0, squares, "z")
            norm_start(1, squares, "x")

        def add(dz, steps, k):
            origin = lax.rem(zh - dz + nz, nz) * nx
            total = None
            for dx in steps:
                block = origin + lax.rem(x - dx + nx, nx)
                product = dot(zb[inst, dz * nx + dx], tiles[idx_s[0, block * cbg + k]])
                total = product if total is None else total + product
            return total

        def group(i, carry):
            dz = order(i)
            take(zb.at[inst, pl.ds(dz * nx + 1, nx - 1)], zb_x.at[inst, dz])
            for k in range(cbg):
                total = add(dz, range(nx), k)
                outp[2 * k] += total[:, :PIECE]
                outp[2 * k + 1] += total[:, PIECE:]
            return carry

        lax.fori_loop(0, nz - 1, group, 0)
        last = ORDER[nz][-1]
        for k in range(cbg):
            total = add(last, [0], k)
            outp[2 * k] += total[:, :PIECE]
            outp[2 * k + 1] += total[:, PIECE:]
        squares = norm_finish(1, squares, "x") if first else norm_finish(3, squares, "row")
        n = 2 if first else 4
        norm_start(n, squares, "col")
        take(zb.at[inst, pl.ds(last * nx + 1, nx - 1)], zb_x.at[inst, last])
        for some in batches(chips[::-1], BACK_BATCH):
            ready = []
            for offset in some:
                k = chip_at(offset, 1)
                total = add(last, range(1, nx), k)
                for h in range(2):
                    value = outp[2 * k + h] + total[:, h * PIECE : (h + 1) * PIECE]
                    slot = slot_of(offset)
                    if any(offset):
                        csend[inst, slot + h] = value.astype(jnp.bfloat16)
                        ready.append((slot, h, 2 * k + h))
                    else:
                        outp[2 * k + h] = value
            for slot, h, piece in ready:
                send(
                    csend.at[inst, slot + h],
                    crecv.at[inst, slot + core],
                    c_send.at[inst],
                    c_sem.at[inst],
                    (r, piece),
                )
        csend[inst, 0] = outp[c + 1 - 2 * core].astype(jnp.bfloat16)
        send(
            csend.at[inst, 0],
            crecv.at[inst, core],
            c_send.at[inst],
            c_sem.at[inst],
            (r, c + 1 - 2 * core),
        )
        if first:
            make_transposed(0, tpd)
        squares = norm_finish(n, squares, "col")
        norm = jnp.sqrt(to_column(squares) + EPSILON)
        prepared = prepare(norm)
        take(crecv.at[inst, pl.ds(1, nc - 1)], c_sem.at[inst])
        total = outp[c] + crecv[inst, 1 - core].astype(jnp.float32)
        for slot in range(2, nc):
            total = total + crecv[inst, slot].astype(jnp.float32)
        return total, norm, prepared

    def forward(inst, vector, n, prepare):
        wrecv[inst, core] = vector.astype(jnp.bfloat16)
        for offset in reversed(chips):
            slot = slot_of(offset)
            chip = chip_at(offset, 1)
            targets = [2 * chip, 2 * chip + 1] if any(offset) else [c + 1 - 2 * core]
            for target in targets:
                send(
                    wrecv.at[inst, core],
                    wrecv.at[inst, slot + core],
                    w_send.at[inst],
                    w_sem.at[inst, slot // 2],
                    (r, target),
                )
        squares = square_sum(vector)
        norm_start(n, squares, "col")

        def arrive(offset):
            slot = slot_of(offset)
            if any(offset):
                take(wrecv.at[inst, pl.ds(slot, 2)], w_sem.at[inst, slot // 2])
            else:
                take(wrecv.at[inst, pl.ds(1 - core, 1)], w_sem.at[inst, 0])
            wfull[slot // 2, :, :PIECE] = wrecv[inst, slot]
            wfull[slot // 2, :, PIECE:] = wrecv[inst, slot + 1]

        def add(block):
            total = None
            for offset in chips:
                k = chip_at(offset, -1)
                product = dot(wfull[slot_of(offset) // 2], ttiles[idx_s[0, block * cbg + k]])
                total = product if total is None else total + product
            return total

        def block_at(dz, dx):
            return lax.rem(zh + dz, nz) * nx + lax.rem(x + dx, nx)

        for offset in chips:
            arrive(offset)
        slots = [dz * nx + dx for dz in reversed(ORDER[nz]) for dx in reversed(ORDER[nx])]
        for some in batches(slots, FORWARD_BATCH):
            for slot in some:
                total = add(block_at(slot // nx, slot % nx))
                if slot % nx == 0:
                    part[slot // nx] = total
                else:
                    s1send[inst, slot] = total.astype(jnp.bfloat16)
            for slot in some:
                if slot % nx:
                    send(
                        s1send.at[inst, slot],
                        s1recv.at[inst, slot],
                        s1_send.at[inst],
                        s1_sem.at[inst, slot // nx],
                        x_peer(slot % nx),
                    )
        squares = norm_finish(n, squares, "col")
        norm_start(n + 1, squares, "row")
        total = None
        for dz in reversed(ORDER[nz]):
            take(s1recv.at[inst, pl.ds(dz * nx + 1, nx - 1)], s1_sem.at[inst, dz])
            total = part[dz]
            for dx in range(1, nx):
                total = total + s1recv[inst, dz * nx + dx].astype(jnp.float32)
            if dz:
                s2send[inst, dz] = total.astype(jnp.bfloat16)
                send(
                    s2send.at[inst, dz],
                    s2recv.at[inst, dz],
                    s2_send.at[inst],
                    s2_sem.at[inst],
                    z_peer(dz),
                )
        squares = norm_finish(n + 1, squares, "row")
        norm = jnp.sqrt(to_column(squares) + EPSILON)
        prepared = prepare(norm)
        take(s2recv.at[inst, pl.ds(1, nz - 1)], s2_sem.at[inst])
        for dz in range(1, nz):
            total = total + s2recv[inst, dz].astype(jnp.float32)
        return total, norm, prepared

    for copy in small:
        copy.wait()
    back, beta0, scale = backward(0, rhs[...], lambda norm: 1.0 / norm, True)
    right_raw0 = back * scale
    forward1, alpha0, (scale, shift) = forward(
        0, right_raw0, 5, lambda norm: (1.0 / norm, (norm / beta0) * rhs[...])
    )
    left_raw1 = forward1 * scale - shift
    first_f[...] = forward1
    back, beta1, (scale, shift) = backward(
        1, left_raw1, lambda norm: (1.0 / norm, (norm / alpha0) * right_raw0), False
    )
    right_raw1 = back * scale - shift
    forward2, alpha1, (scale, shift) = forward(
        1, right_raw1, 7, lambda norm: (1.0 / norm, (norm / beta1) * left_raw1)
    )
    left_raw2 = forward2 * scale - shift

    squares = square_sum(left_raw2)
    norm_start(9, squares, "core")
    squares = norm_finish(9, squares, "core")
    norm_start(10, squares, "chips")
    rho_bar = alpha0
    phi_bar = beta0
    rho_value = jnp.sqrt(rho_bar * rho_bar + beta1 * beta1)
    cosine = rho_bar / rho_value
    sine_value = beta1 / rho_value
    theta_value = sine_value * alpha1
    step0 = cosine * phi_bar / rho_value
    turn0 = theta_value / rho_value
    rho_bar = -cosine * alpha1
    phi_bar = sine_value * phi_bar
    squares = norm_finish(10, squares, "chips")
    beta2 = jnp.sqrt(to_column(squares) + EPSILON)
    rho_value = jnp.sqrt(rho_bar * rho_bar + beta2 * beta2)
    step1 = rho_bar / rho_value * phi_bar / rho_value
    weight0 = step0 - step1 * turn0
    weight0 = weight0 / alpha0
    weight1 = step1 / alpha1
    sol_out[...] = weight0 * right_raw0 + weight1 * right_raw1
    res_out[...] = rhs[...] - weight0 * first_f[...] - weight1 * forward2

    for inst in range(2):
        take(zb.at[inst, pl.ds(1, nr - 1)], zb_send.at[inst])
        take(s1recv.at[inst, pl.ds(0, nz * (nx - 1))], s1_send.at[inst])
        take(s2recv.at[inst, pl.ds(1, nz - 1)], s2_send.at[inst])
        take(crecv.at[inst, pl.ds(1, nc - 1)], c_send.at[inst])
        take(wrecv.at[inst, pl.ds(1, nc - 1)], w_send.at[inst])
    kinds = ("z", "x", "col", "row", "col", "col", "row", "col", "row", "core")
    for n, kind in enumerate(kinds):
        take(nrecv.at[n, pl.ds(0, len(peers[kind]))], n_send.at[n])
    take(frecv.at[pl.ds(0, len(peers["chips"]))], n_send.at[10])


def place(solution, residual, sol_out, res_out):
    sol_out[:, 0, :] = solution[...]
    res_out[:, 0, :] = residual[...]


def local(dims, right_side, tile_values, tile_rows, tile_cols, tile_count):
    nz, nx, nc, cbg, tpd, sides = dims
    nr = nz * nx
    bf16, f32, i32 = jnp.bfloat16, jnp.float32, jnp.int32
    vmem = pl.BlockSpec(memory_space=pltpu.VMEM)
    dma = pltpu.SemaphoreType.DMA
    solution, residual = pl.pallas_call(
        functools.partial(kernel, dims),
        out_shape=(
            jax.ShapeDtypeStruct((sides, PIECE), f32),
            jax.ShapeDtypeStruct((sides, TILE), f32),
        ),
        in_specs=[pl.BlockSpec(memory_space=pltpu.HBM)] * 5,
        out_specs=(vmem, vmem),
        scratch_shapes=[
            pltpu.SMEM((1, 1, tpd), i32),
            pltpu.SMEM((1, 1, tpd), i32),
            pltpu.SMEM((1, 1), i32),
            pltpu.VMEM((sides, TILE), f32),
            pltpu.VMEM((tpd + 1, TILE, TILE), bf16),
            pltpu.VMEM((tpd + 1, TILE, TILE), bf16),
            pltpu.VMEM((8, 128), i32),
            pltpu.SMEM((8, 128), i32),
            pltpu.VMEM((2, nr, sides, TILE), bf16),
            pltpu.VMEM((2, nr, sides, TILE), bf16),
            pltpu.VMEM((2, nr, sides, TILE), bf16),
            pltpu.VMEM((2, nz, sides, TILE), bf16),
            pltpu.VMEM((2, nz, sides, TILE), bf16),
            pltpu.VMEM((nz, sides, TILE), f32),
            pltpu.VMEM((2, nc, sides, PIECE), bf16),
            pltpu.VMEM((2, nc, sides, PIECE), bf16),
            pltpu.VMEM((2, nc, sides, PIECE), bf16),
            pltpu.VMEM((cbg, sides, TILE), bf16),
            pltpu.VMEM((nc, sides, PIECE), f32),
            pltpu.VMEM((sides, TILE), f32),
            pltpu.VMEM((16, 128), f32),
            pltpu.VMEM((10, max(nr, nc), 128), f32),
            pltpu.VMEM((nr * nc // 2, 128), f32),
            dma,
            dma((3,)),
            dma,
            dma,
            dma((2,)),
            dma((2, nz, 2)),
            dma((2, nz)),
            dma((2,)),
            dma((2, nz)),
            dma((2,)),
            dma((2,)),
            dma((2,)),
            dma((2,)),
            dma((2,)),
            dma((2, cbg)),
            dma((11,)),
            dma((11,)),
        ],
        compiler_params=pltpu.CompilerParams(
            collective_id=0, has_side_effects=True, vmem_limit_bytes=62 * 2**20
        ),
        name="lsqr",
    )(tile_rows, tile_cols, tile_count, right_side, tile_values)
    return pl.pallas_call(
        place,
        out_shape=(
            jax.ShapeDtypeStruct((sides, 1, PIECE), f32),
            jax.ShapeDtypeStruct((sides, 1, TILE), f32),
        ),
        in_specs=[vmem, vmem],
        out_specs=(vmem, vmem),
        name="place",
    )(solution, residual)


def solution(mesh):
    in_specs = (
        P(None, "col", "row"),
        P("row", "col", None, None, None),
        P("row", "col", None),
        P("row", "col", None),
        P("row", "col"),
    )
    out_specs = (P(None, "row", "col"), P(None, "col", "row"))
    nr, nc = mesh.shape["row"], mesh.shape["col"]
    nz = 4 if nr == 16 else 2

    def program(right_side, tile_values, tile_rows, tile_cols, tile_count):
        dims = (nz, nr // nz, nc, nc * PIECE // TILE, tile_values.shape[2], right_side.shape[0])
        return jax.shard_map(
            functools.partial(local, dims),
            mesh=mesh,
            in_specs=in_specs,
            out_specs=out_specs,
            check_vma=False,
        )(right_side, tile_values, tile_rows, tile_cols, tile_count)

    return program
```
